32 devices in a mesh: region: 4 (over y, core), member: 8 (over z, x).
Axes of the slice: x: 2, y: 2, z: 4, core: 2. Of those that a mesh axis runs over, the one named last changes fastest.
Arguments:
- interface_load: float32 [512, 1024], P(('region', 'member')), may hold values from -23 to 23
- schur_values: float32 [512, 16, 4096], P(('region', 'member')), may hold values from -0.04 to 2.04, as said below
- schur_columns: int32 [512, 16], P(('region', 'member')), may hold values from 0 to 511, as said below
- coupling: float32 [64, 1024, 512], P(('region', 'member')), may hold values from -0.25 to 0.25
- layer_inverse: float32 [64, 1024, 1024], P(('region', 'member')), may hold values from -0.1875 to 0.1875
- interior_load: float32 [64, 16, 1024], P(('region', 'member')), may hold values from -6 to 6
- adjacency: int32 [64, 8], P(('region', 'member')), may hold values from 0 to 511, as said below
- live_counts: int32 [64], P(('region', 'member')), may hold values from 4 to 8, as said below
Outputs:
- solution: float32 [512, 1024], P(('region', 'member'))
- residual: float32 [512, 1024], P(('region', 'member'))
- interior: float32 [64, 16, 1024], P(('region', 'member'))
The draws below stay inside these ranges and needn't reach their ends.
Inputs may be any that keep to these rules, and one draw needn't show every extreme that they name: `schur_columns`: block row i of region g = i // 128 stores its own block in slot 0; slot 1 holds a block of region g - 1 and slot 2 one of region g + 1 (of region g itself at the ends), each such block named by exactly one row of region g; the other slots name blocks of regions g - 1 to g + 1 that exist. Call the blocks b with (b % 128) // 16 = m the blocks of member index m; the rows of one device name at most 32 distinct blocks of any one member index, and exactly 32 for some member index on every device of a region other than the first and last. `schur_values`: the slot 0 block of each row is 2 times the identity plus small entries; all other entries are small. `adjacency`: the substructures of device d (those with index // 2 equal to d) name blocks of regions r - 1 to r + 1 that exist, where r = d // 8; slots past the live count hold such blocks too. `live_counts`: every substructure with an even index has all 8 slots live.
All inputs are finite; a program needn't handle non-finite values.
Results may differ from the reference program's by a relative error of at most 0.0003.
Values sent between devices are 32-bit elements; how exact they have to be, the bound alone decides.
A program may use at most 128 MiB of HBM per device.

```python
import jax
import jax.numpy as jnp
from jax import lax

NB = 64
CASES = 16
ITERS = 2
K_SLOTS = 16
A_PAD = 8
IB_DEV = 16
SUB_DEV = 2
NI = 1024
IB_REG = 128
IB_ALL = 512
SUBS = 64
N_REGION = 4
N_MEMBER = 8


def draw_interface_load(key, part):
    key = jax.random.fold_in(key, 5)
    row_ids = jnp.arange(IB_ALL, dtype=jnp.float32)[:, None]
    ramp = 0.6 + 1.2 * row_ids / max(IB_ALL - 1, 1)
    rough = jnp.exp(jax.random.uniform(jax.random.fold_in(key, 1), (IB_ALL, 1), jnp.float32, -1.15, 1.15))
    values = jnp.clip(jax.random.normal(key, (IB_ALL, CASES * NB), jnp.float32), -4.0, 4.0)
    return (values * ramp * rough).astype(jnp.float32)


def draw_schur_values(key, part):
    key = jax.random.fold_in(key, 7)
    small = jax.random.uniform(key, (IB_ALL, K_SLOTS, NB * NB), jnp.float32, -0.04, 0.04)
    flat = jnp.arange(NB * NB, dtype=jnp.int32)
    diagonal = (flat // NB == flat % NB).astype(jnp.float32)
    slot_zero = (jnp.arange(K_SLOTS, dtype=jnp.int32) == 0).astype(jnp.float32)
    return (small + 2.0 * slot_zero[None, :, None] * diagonal[None, None, :]).astype(jnp.float32)


def draw_schur_columns(key, part):
    key = jax.random.fold_in(key, 11)
    half = (IB_DEV + 1) // 2
    row_ids = jnp.arange(IB_ALL, dtype=jnp.int32)[:, None]
    region_ids = row_ids // IB_REG
    within = row_ids % IB_REG
    own_member = within // IB_DEV
    offset = within % IB_DEV
    first_shift = jax.random.randint(jax.random.fold_in(key, 1), (N_REGION,), 1, N_MEMBER, dtype=jnp.int32)
    extra = jax.random.randint(jax.random.fold_in(key, 2), (N_REGION,), 1, N_MEMBER - 1, dtype=jnp.int32)
    second_shift = 1 + (first_shift - 1 + extra) % (N_MEMBER - 1)
    member_one = (own_member + first_shift[region_ids[:, 0]][:, None]) % N_MEMBER
    member_two = (own_member + second_shift[region_ids[:, 0]][:, None]) % N_MEMBER
    below_region = jnp.where(region_ids > 0, region_ids - 1, region_ids)
    above_region = jnp.where(region_ids < N_REGION - 1, region_ids + 1, region_ids)
    below = below_region * IB_REG + member_one * IB_DEV + offset
    above = above_region * IB_REG + member_two * IB_DEV + offset
    third = region_ids * IB_REG + member_one * IB_DEV + offset % half
    fourth = above_region * IB_REG + member_one * IB_DEV + offset % half
    lowest = jnp.maximum(region_ids - 1, 0)
    count_regions = jnp.minimum(region_ids + 2, N_REGION) - lowest
    bits_region = jax.random.randint(jax.random.fold_in(key, 3), (IB_ALL, K_SLOTS), 0, 1 << 20, dtype=jnp.int32)
    bits_member = jax.random.randint(jax.random.fold_in(key, 4), (IB_ALL, K_SLOTS), 0, N_MEMBER, dtype=jnp.int32)
    bits_offset = jax.random.randint(jax.random.fold_in(key, 5), (IB_ALL, K_SLOTS), 0, half, dtype=jnp.int32)
    anywhere = (lowest + bits_region % count_regions) * IB_REG + bits_member * IB_DEV + bits_offset
    slot_ids = jnp.arange(K_SLOTS, dtype=jnp.int32)[None, :]
    picked = jnp.where(slot_ids == 0, row_ids, jnp.where(slot_ids == 1, below, jnp.where(slot_ids == 2, above, jnp.where(slot_ids == 3, third, jnp.where(slot_ids == 4, fourth, anywhere)))))
    return picked.astype(jnp.int32)


def draw_adjacency(key, part):
    key = jax.random.fold_in(key, 13)
    sub_ids = jnp.arange(SUBS, dtype=jnp.int32)[:, None]
    region_ids = sub_ids // SUB_DEV // N_MEMBER
    lowest = jnp.maximum(region_ids - 1, 0) * IB_REG
    highest = jnp.minimum(region_ids + 2, N_REGION) * IB_REG
    random_bits = jax.random.randint(key, (SUBS, A_PAD), 0, 1 << 20, dtype=jnp.int32)
    return (lowest + random_bits % (highest - lowest)).astype(jnp.int32)


def draw_live_counts(key, part):
    key = jax.random.fold_in(key, 17)
    counts = jax.random.randint(key, (SUBS,), (A_PAD + 1) // 2, A_PAD + 1, dtype=jnp.int32)
    sub_ids = jnp.arange(SUBS, dtype=jnp.int32)
    return jnp.where(sub_ids % 2 == 0, A_PAD, counts).astype(jnp.int32)


def block_scale(stream_key, shape, cuts, smallest, high):
    def one(position, shards_of):
        draws = jax.random.uniform(jax.random.fold_in(jax.random.fold_in(stream_key, 6), position), (shards_of,), jnp.float32, smallest / len(cuts), high / len(cuts))
        return jnp.repeat(jnp.exp(draws), shape[position] // shards_of).reshape((-1,) + (1,) * (len(shape) - position - 1))

    level = one(*cuts[0])
    for cut in cuts[1:]:
        level = level * one(*cut)
    return level


def noise(key, extent, scale, limit, pieces=(), kind=jnp.bfloat16):
    values = scale * jax.random.normal(key, extent, jnp.float32)
    if pieces:
        values = values * block_scale(key, extent, pieces, -0.22, 0.18)
    return jnp.clip(values, -limit, limit).astype(kind)


def setup_inputs(seed: int = 0) -> dict:
    streams_of = jax.random.split(jax.random.key(seed), 9)
    return {
        "interface_load": draw_interface_load(jax.random.fold_in(streams_of[8], 71), 0),
        "schur_values": draw_schur_values(jax.random.fold_in(streams_of[8], 71), 0),
        "schur_columns": draw_schur_columns(jax.random.fold_in(streams_of[8], 71), 0),
        "coupling": noise(streams_of[3], (SUBS, NI, A_PAD * NB), (A_PAD * NB) ** -0.5, 0.25, ((0, 32),), jnp.float32),
        "layer_inverse": noise(streams_of[4], (SUBS, NI, NI), NI ** -0.5, 0.1875, ((0, 32),), jnp.float32),
        "interior_load": noise(streams_of[5], (SUBS, CASES, NI), 1.0, 6.0, ((0, 32),), jnp.float32),
        "adjacency": draw_adjacency(jax.random.fold_in(streams_of[8], 71), 0),
        "live_counts": draw_live_counts(jax.random.fold_in(streams_of[8], 71), 0),
    }


HIGHEST_MODE = lax.Precision.HIGHEST


def apply_schur(values, column_ids, field):
    blocks = field.reshape(field.shape[0], CASES, NB)[column_ids]
    matrices = values.reshape(values.shape[0], values.shape[1], NB, NB)
    result = jnp.einsum("ikrq,ikcq->icr", matrices, blocks, precision=HIGHEST_MODE)
    return result.reshape(result.shape[0], CASES * NB)


def case_partial(left, right):
    return jnp.sum((left * right).reshape(-1, CASES, NB), axis=(0, 2))


def widen(factor):
    return jnp.repeat(factor, NB)[None, :]


def recover(field, slot_ids, live_counts, coupling, layer_inverse, interior_load):
    picked = field.reshape(field.shape[0], CASES, NB)[slot_ids]
    positions = jnp.arange(picked.shape[1], dtype=jnp.int32)
    live_mask = (positions[None, :] < live_counts[:, None]).astype(jnp.float32)
    picked = picked * live_mask[:, :, None, None]
    matrices = coupling.reshape(coupling.shape[0], coupling.shape[1], -1, NB)
    reduced = interior_load - jnp.einsum("snaq,sacq->scn", matrices, picked, precision=HIGHEST_MODE)
    return jnp.einsum("snm,scm->scn", layer_inverse, reduced, precision=HIGHEST_MODE)


def reference(interface_load, schur_values, schur_columns, coupling, layer_inverse, interior_load, adjacency, live_counts):
    solution = jnp.zeros_like(interface_load)
    residual = interface_load
    direction = interface_load
    norm_now = case_partial(residual, residual)
    for iteration in range(ITERS):
        image = apply_schur(schur_values, schur_columns, direction)
        step_size = norm_now / case_partial(direction, image)
        solution = solution + widen(step_size) * direction
        residual = residual - widen(step_size) * image
        if iteration + 1 < ITERS:
            norm_next = case_partial(residual, residual)
            direction = residual + widen(norm_next / norm_now) * direction
            norm_now = norm_next
    interior = recover(solution, adjacency, live_counts, coupling, layer_inverse, interior_load)
    return (solution, residual, interior)
```

```python
import functools

import jax
import jax.numpy as jnp
from jax import lax
from jax.experimental import pallas as pl
from jax.experimental.pallas import tpu as pltpu
from jax.sharding import PartitionSpec as P

NB = 64
CASES = 16
HIGHEST_MODE = lax.Precision.HIGHEST
MESH = pl.DeviceIdType.MESH


def exchange_kernel(regions, outer, inner, gather, sums, *refs):
    refs = list(refs)
    block_ref = refs.pop(0) if gather else None
    part_ref = refs.pop(0) if sums else None
    win_ref = refs.pop(0) if gather else None
    total_ref = refs.pop(0) if sums else None
    if gather:
        own_sem, recv_sem, line_sem, side_sem, region_sem = refs[:5]
        refs = refs[5:]
    if sums:
        parts, rows, member_send, member_recv, row_send, row_recv = refs
    members = outer * inner
    g = lax.axis_index("region")
    m = lax.axis_index("member")
    a = m // inner
    b = m % inner
    has_low = g > 0
    has_high = g < regions - 1
    barrier = pltpu.get_barrier_semaphore()

    def greet(region, member):
        pl.semaphore_signal(barrier, inc=1, device_id=(region, member), device_id_type=MESH)

    if sums:
        for step in range(1, members):
            greet(g, lax.rem(m + step, members))
        for step in range(1, regions):
            greet(lax.rem(g + step, regions), m)
        pl.semaphore_wait(barrier, members - 1 + regions - 1)
    else:
        for step in range(1, outer):
            greet(g, lax.rem(a + step, outer) * inner + b)
        for step in range(1, inner):
            greet(g, a * inner + lax.rem(b + step, inner))

        @pl.when(has_low)
        def _():
            greet(g - 1, m)

        @pl.when(has_high)
        def _():
            greet(g + 1, m)

        amount = outer - 1 + inner - 1 + jnp.where(has_low, 1, 0) + jnp.where(has_high, 1, 0)
        pl.semaphore_wait(barrier, amount)

    def remote(source, target, send, recv, region, member):
        return pltpu.make_async_remote_copy(
            src_ref=source, dst_ref=target, send_sem=send, recv_sem=recv,
            device_id=(region, member), device_id_type=MESH,
        )

    if sums:
        member_copies = []
        for step in range(1, members):
            copy = remote(part_ref, parts.at[m], member_send.at[step], member_recv.at[m],
                          g, lax.rem(m + step, members))
            copy.start()
            member_copies.append(copy)

    sent = []

    def slot(rel, row, column):
        return win_ref.at[rel, row, column]

    def line_copy(step):
        return remote(block_ref, slot(1, a, b), line_sem.at[step], recv_sem.at[1, a, b],
                      g, lax.rem(a + step, outer) * inner + b)

    def side_copy(source, row, step):
        return remote(source, slot(1, row, b), side_sem.at[row, step], recv_sem.at[1, row, b],
                      g, a * inner + lax.rem(b + step, inner))

    def region_copy(source, row, column, up):
        rel = 0 if up else 2
        return remote(source, slot(rel, row, column), region_sem.at[rel // 2, row, column],
                      recv_sem.at[rel, row, column], g + 1 if up else g - 1, m)

    def spread_regions(source, row, column):
        @pl.when(has_high)
        def _():
            region_copy(source, row, column, True).start()

        @pl.when(has_low)
        def _():
            region_copy(source, row, column, False).start()

    def await_slot(rel, row, column):
        remote(slot(rel, row, column), slot(rel, row, column), own_sem.at[1], recv_sem.at[rel, row, column], g, m).wait_recv()

    if gather:
        for step in range(1, outer):
            copy = line_copy(step)
            copy.start()
            sent.append(copy)
        for step in range(1, inner):
            copy = side_copy(block_ref, a, step)
            copy.start()
            sent.append(copy)
        spread_regions(block_ref, a, b)
        own = pltpu.make_async_copy(block_ref, slot(1, a, b), own_sem.at[0])
        own.start()

    if sums:
        for step in range(1, members):
            other = lax.rem(m + step, members)
            remote(part_ref, parts.at[other], member_send.at[step], member_recv.at[other], g, other).wait_recv()
        total = jnp.zeros_like(part_ref[...])
        for other in range(members):
            total = total + jnp.where(m == other, part_ref[...], parts[other])
        rows[g] = total
        row_copies = []
        for step in range(1, regions):
            copy = remote(rows.at[g], rows.at[g], row_send.at[step], row_recv.at[g],
                          lax.rem(g + step, regions), m)
            copy.start()
            row_copies.append(copy)

    if gather:
        for step in range(1, outer):
            row = lax.rem(a + step, outer)
            await_slot(1, row, b)
            for side in range(1, inner):
                copy = side_copy(slot(1, row, b), row, side)
                copy.start()
                sent.append(copy)
            spread_regions(slot(1, row, b), row, b)
        for step in range(outer):
            row = lax.rem(a + step, outer)
            for side in range(1, inner):
                column = lax.rem(b + side, inner)
                await_slot(1, row, column)
                spread_regions(slot(1, row, column), row, column)

    if sums:
        for step in range(1, regions):
            other = lax.rem(g + step, regions)
            remote(rows.at[other], rows.at[other], row_send.at[step], row_recv.at[other], other, m).wait_recv()
        total = rows[0]
        for other in range(1, regions):
            total = total + rows[other]
        total_ref[...] = total
        for copy in member_copies + row_copies:
            copy.wait_send()

    if gather:
        own.wait()
        for copy in sent:
            copy.wait_send()
        for row in range(outer):
            for column in range(inner):
                @pl.when(has_low)
                def _():
                    await_slot(0, row, column)
                    region_copy(slot(1, row, column), row, column, False).wait_send()

                @pl.when(has_high)
                def _():
                    await_slot(2, row, column)
                    region_copy(slot(1, row, column), row, column, True).wait_send()


def exchange(number, regions, members, block=None, part=None):
    outer = 4 if members % 4 == 0 else members
    inner = members // outer
    gather, sums = block is not None, part is not None
    operands, shapes, scratch = [], [], []
    if gather:
        operands.append(block)
        shapes.append(jax.ShapeDtypeStruct((3, outer, inner) + block.shape, jnp.float32))
        scratch += [
            pltpu.SemaphoreType.DMA((2,)),
            pltpu.SemaphoreType.DMA((3, outer, inner)),
            pltpu.SemaphoreType.DMA((outer,)),
            pltpu.SemaphoreType.DMA((outer, inner)),
            pltpu.SemaphoreType.DMA((2, outer, inner)),
        ]
    if sums:
        operands.append(part)
        shapes.append(jax.ShapeDtypeStruct(part.shape, jnp.float32))
        scratch += [
            pltpu.VMEM((members,) + part.shape, jnp.float32),
            pltpu.VMEM((regions,) + part.shape, jnp.float32),
            pltpu.SemaphoreType.DMA((members,)),
            pltpu.SemaphoreType.DMA((members,)),
            pltpu.SemaphoreType.DMA((regions,)),
            pltpu.SemaphoreType.DMA((regions,)),
        ]
    vmem = pl.BlockSpec(memory_space=pltpu.VMEM)
    return pl.pallas_call(
        functools.partial(exchange_kernel, regions, outer, inner, gather, sums),
        out_shape=tuple(shapes),
        in_specs=[vmem] * len(operands),
        out_specs=tuple([vmem] * len(shapes)),
        scratch_shapes=scratch,
        compiler_params=pltpu.CompilerParams(
            collective_id=number, has_side_effects=True, vmem_limit_bytes=32 * 2**20
        ),
    )(*operands)


def apply_schur(matrices, column_ids, field):
    blocks = field.reshape(-1, CASES, NB)[column_ids]
    result = jnp.einsum("ikrq,ikcq->icr", matrices, blocks, precision=HIGHEST_MODE)
    return result.reshape(result.shape[0], CASES * NB)


def case_partial(left, right):
    return jnp.sum((left * right).reshape(-1, CASES, NB), axis=(0, 2))


def widen(factor):
    return jnp.repeat(factor, NB)[None, :]


def pad_parts(*parts):
    return jnp.pad(jnp.stack(parts), ((0, 8 - len(parts)), (0, 128 - CASES)))


def body(interface_load, schur_values, schur_columns, coupling, layer_inverse, interior_load, adjacency, live_counts):
    block_rows = interface_load.shape[0]
    members = lax.axis_size("member")
    regions = lax.axis_size("region")
    region_rows = block_rows * members
    region_index = lax.axis_index("region")

    def locate(global_ids):
        return global_ids - (region_index - 1) * region_rows

    columns = locate(schur_columns)
    load = interface_load
    matrices = schur_values.reshape(block_rows, -1, NB, NB)

    (load_window,) = exchange(0, regions, members, block=load)
    load_window = load_window.reshape(-1, CASES * NB)
    image = apply_schur(matrices, columns, load_window)
    part = pad_parts(case_partial(load, load), case_partial(load, image))
    image_window, first = exchange(1, regions, members, block=image, part=part)
    image_window = image_window.reshape(-1, CASES * NB)
    norm, curve = first[0, :CASES], first[1, :CASES]
    step = norm / curve
    residual = load - widen(step) * image
    residual_window = load_window - widen(step) * image_window
    image_two = apply_schur(matrices, columns, residual_window)
    part = pad_parts(
        case_partial(residual, residual),
        case_partial(residual, image_two),
        case_partial(residual, image) + case_partial(load, image_two),
    )
    (second,) = exchange(2, regions, members, part=part)
    norm_next, square, cross = (second[row, :CASES] for row in range(3))
    ratio = norm_next / norm
    step_two = norm_next / (square + ratio * (cross + ratio * curve))

    along = step + step_two * ratio
    result = widen(along) * load + widen(step_two) * residual
    final = residual - widen(step_two) * (image_two + widen(ratio) * image)

    ids = locate(adjacency)
    picked = (along[None, None, :, None] * load_window.reshape(-1, CASES, NB)[ids]
              + step_two[None, None, :, None] * residual_window.reshape(-1, CASES, NB)[ids])
    positions = jnp.arange(picked.shape[1], dtype=jnp.int32)
    picked = jnp.where((positions[None, :] < live_counts[:, None])[:, :, None, None], picked, 0.0)
    groups = coupling.reshape(coupling.shape[0], coupling.shape[1], -1, NB)
    reduced = interior_load - jnp.einsum("snaq,sacq->scn", groups, picked, precision=HIGHEST_MODE)
    interior = jnp.einsum("snm,scm->scn", layer_inverse, reduced, precision=HIGHEST_MODE)
    return (result, final, interior)


def solution(mesh):
    in_specs = (
        P(("region", "member"), None),
        P(("region", "member"), None, None),
        P(("region", "member"), None),
        P(("region", "member"), None, None),
        P(("region", "member"), None, None),
        P(("region", "member"), None, None),
        P(("region", "member"), None),
        P(("region", "member")),
    )
    out_specs = (
        P(("region", "member"), None),
        P(("region", "member"), None),
        P(("region", "member"), None, None),
    )
    return jax.shard_map(body, mesh=mesh, in_specs=in_specs, out_specs=out_specs, check_vma=False)
```

```python
import functools

import jax
import jax.numpy as jnp
from jax import lax
from jax.experimental import pallas as pl
from jax.experimental.pallas import tpu as pltpu
from jax.sharding import PartitionSpec as P

NB = 64
CASES = 16
LANES = 2 * NB
MESH = pl.DeviceIdType.MESH
F32 = jnp.float32
BF16 = jnp.bfloat16


def split(value):
    high = value.astype(BF16)
    return high, (value - high.astype(F32)).astype(BF16)


def dot_rows(left, right, precision=None):
    return lax.dot_general(left, right, (((1,), (1,)), ((), ())), precision=precision, preferred_element_type=F32)


def fused_kernel(regions, outer, inner, cols, adj, live, load_ref, iload_ref, values_hbm, coupling_hbm, inverse_hbm,
                 result_ref, final_ref, interior_ref,
                 win_load, win_image, second_ref, tiles_ref, values_ref, xx, raw, coup, coup_h, coup_l, inv, inv_h, inv_l, base, parts, rows,
                 value_sem, big_sem, recv_sem, line_sem, side_sem, region_sem,
                 member_send, member_recv, row_send, row_recv):
    members = outer * inner
    windows = (win_load, win_image)
    block_rows = cols.shape[0]
    slots = cols.shape[1]
    pairs = block_rows // 2
    subs, interior_size = iload_ref.shape[0], iload_ref.shape[2]
    groups = values_hbm.shape[2] // LANES
    octets = slots // 8
    g = lax.axis_index("region")
    m = lax.axis_index("member")
    a = m // inner
    b = m % inner
    has_low = g > 0
    has_high = g < regions - 1
    barrier = pltpu.get_barrier_semaphore()
    lane = lax.broadcasted_iota(jnp.int32, (CASES, LANES), 1)
    upper = lane // NB

    def value_copy(octet, group):
        return pltpu.make_async_copy(
            values_hbm.at[:, pl.ds(octet * 8, 8), pl.ds(pl.multiple_of(group * LANES, LANES), LANES)],
            tiles_ref.at[:, octet, group], value_sem.at[octet, group])

    def greet(region, member):
        pl.semaphore_signal(barrier, inc=1, device_id=(region, member), device_id_type=MESH)

    for step in range(1, members):
        greet(g, lax.rem(m + step, members))
    for step in range(1, regions):
        greet(lax.rem(g + step, regions), m)

    for octet in range(octets):
        def start_values(group, carry):
            value_copy(octet, group).start()
            return carry
        lax.fori_loop(0, groups, start_values, 0)
    big = [pltpu.make_async_copy(coupling_hbm, coup, big_sem.at[0]),
           pltpu.make_async_copy(inverse_hbm, inv, big_sem.at[1])]
    for copy in big:
        copy.start()

    pl.semaphore_wait(barrier, members - 1 + regions - 1)

    def remote(source, target, send, recv, region, member):
        return pltpu.make_async_remote_copy(
            src_ref=source, dst_ref=target, send_sem=send, recv_sem=recv,
            device_id=(region, member), device_id_type=MESH,
        )

    def slot(turn, rel, row, column):
        first = ((rel * outer + row) * inner + column) * pairs
        return windows[turn].at[pl.ds(first, pairs)]

    def line_copy(turn, step):
        here = slot(turn, 1, a, b)
        return remote(here, here, line_sem.at[turn, step], recv_sem.at[turn, 1, a, b],
                      g, lax.rem(a + step, outer) * inner + b)

    def side_copy(turn, row, step):
        here = slot(turn, 1, row, b)
        return remote(here, here, side_sem.at[turn, row, step], recv_sem.at[turn, 1, row, b],
                      g, a * inner + lax.rem(b + step, inner))

    def region_copy(turn, row, column, up):
        rel = 0 if up else 2
        return remote(slot(turn, 1, row, column), slot(turn, rel, row, column),
                      region_sem.at[turn, rel // 2, row, column],
                      recv_sem.at[turn, rel, row, column], g + 1 if up else g - 1, m)

    def spread_regions(turn, row, column):
        @pl.when(has_high)
        def _():
            region_copy(turn, row, column, True).start()

        @pl.when(has_low)
        def _():
            region_copy(turn, row, column, False).start()

    def await_slot(turn, rel, row, column):
        here = slot(turn, rel, row, column)
        remote(here, here, line_sem.at[turn, 0], recv_sem.at[turn, rel, row, column], g, m).wait_recv()

    def send_own(turn):
        for step in range(1, outer):
            line_copy(turn, step).start()
        for step in range(1, inner):
            side_copy(turn, a, step).start()
        spread_regions(turn, a, b)

    def forward_line(turn):
        for step in range(1, outer):
            row = lax.rem(a + step, outer)
            await_slot(turn, 1, row, b)
            for side in range(1, inner):
                side_copy(turn, row, side).start()
            spread_regions(turn, row, b)

    def forward_side(turn):
        for step in range(outer):
            row = lax.rem(a + step, outer)
            for side in range(1, inner):
                column = lax.rem(b + side, inner)
                await_slot(turn, 1, row, column)
                spread_regions(turn, row, column)

    def await_regions(turn):
        for row in range(outer):
            for column in range(inner):
                @pl.when(has_low)
                def _():
                    await_slot(turn, 0, row, column)

                @pl.when(has_high)
                def _():
                    await_slot(turn, 2, row, column)

    def finish_sends(turn):
        for step in range(1, outer):
            line_copy(turn, step).wait_send()
        for row in range(outer):
            for step in range(1, inner):
                side_copy(turn, row, step).wait_send()
            for column in range(inner):
                @pl.when(has_low)
                def _():
                    region_copy(turn, row, column, False).wait_send()

                @pl.when(has_high)
                def _():
                    region_copy(turn, row, column, True).wait_send()

    def member_copy(turn, step):
        here = parts.at[turn, m]
        return remote(here, here, member_send.at[turn, step], member_recv.at[turn, m], g, lax.rem(m + step, members))

    def row_copy(turn, step):
        here = rows.at[turn, g]
        return remote(here, here, row_send.at[turn, step], row_recv.at[turn, g], lax.rem(g + step, regions), m)

    def sum_start(turn, products):
        packed = jnp.zeros((CASES, LANES), F32)
        for place, product in enumerate(products):
            packed = jnp.where(lane == place, jnp.sum(product, axis=1, keepdims=True), packed)
        parts[turn, m] = packed
        for step in range(1, members):
            member_copy(turn, step).start()

    def sum_middle(turn):
        for step in range(1, members):
            other = lax.rem(m + step, members)
            here = parts.at[turn, other]
            remote(here, here, member_send.at[turn, 0], member_recv.at[turn, other], g, other).wait_recv()
        total = parts[turn, 0]
        for other in range(1, members):
            total = total + parts[turn, other]
        rows[turn, g] = total
        for step in range(1, regions):
            row_copy(turn, step).start()

    def sum_end(turn, count):
        for step in range(1, regions):
            other = lax.rem(g + step, regions)
            here = rows.at[turn, other]
            remote(here, here, row_send.at[turn, 0], row_recv.at[turn, other], other, m).wait_recv()
        total = rows[turn, 0]
        for other in range(1, regions):
            total = total + rows[turn, other]
        for step in range(1, members):
            member_copy(turn, step).wait_send()
        for step in range(1, regions):
            row_copy(turn, step).wait_send()
        return [jnp.sum(jnp.where(lane == place, total, 0.0), axis=1, keepdims=True) for place in range(count)]

    first_id = (g - 1) * (block_rows * members)

    def prepare_values():
        for octet in range(octets):
            def wait_values(group, carry):
                value_copy(octet, group).wait()
                return carry
            lax.fori_loop(0, groups, wait_values, 0)
        flat = tiles_ref.reshape(block_rows * octets * groups * 8, LANES)

        def one(i, carry):
            for k in range(slots):
                start = (i * octets + k // 8) * (groups * 8) + k % 8
                high, low = split(flat[pl.ds(start, groups, stride=8), :])
                values_ref[i, 0:groups, k * LANES:(k + 1) * LANES] = high
                values_ref[i, groups:2 * groups, k * LANES:(k + 1) * LANES] = low
            return carry
        lax.fori_loop(0, block_rows, one, 0)

    def doubled(fetch, block):
        local = jnp.clip(block - first_id, 0, 3 * members * block_rows - 1)
        tile = fetch(lax.shift_right_logical(local, 1))
        kept = jnp.where(upper == lax.bitwise_and(local, 1), tile, 0.0)
        return kept + pltpu.roll(kept, NB, 1)

    def apply_schur(fetch):
        def one(t, carry):
            for parity in range(2):
                i = 2 * t + parity
                for k in range(slots):
                    both = doubled(fetch, cols[i, k])
                    place = slice(k * LANES, (k + 1) * LANES)
                    for p in range(2):
                        high, low = split(jnp.where(upper == p, both, 0.0))
                        xx[i, p * CASES:(p + 1) * CASES, place] = high
                        xx[i, (2 + p) * CASES:(3 + p) * CASES, place] = low
            for parity in range(2):
                i = 2 * t + parity
                product = dot_rows(xx[i], values_ref[i])
                product = product[0:2 * CASES] + product[2 * CASES:4 * CASES]
                for p in range(2):
                    raw[parity, p, t] = product[p * CASES:(p + 1) * CASES]
            return carry
        lax.fori_loop(0, pairs, one, 0)
        place = lax.broadcasted_iota(jnp.int32, (LANES, 2 * groups), 0)
        source = lax.broadcasted_iota(jnp.int32, (LANES, 2 * groups), 1) % groups
        total = jnp.zeros((pairs * CASES, LANES), F32)
        for parity in range(2):
            for p in range(2):
                chosen = (place == parity * NB + 2 * source + p).astype(F32)
                total = total + dot_rows(raw[parity, p].reshape(pairs * CASES, 2 * groups), chosen, lax.Precision.HIGHEST)
        return total.reshape(pairs, CASES, LANES)

    def prepare_recovery():
        for copy in big:
            copy.wait()
        for source, high_ref, low_ref in ((coup, coup_h, coup_l), (inv, inv_h, inv_l)):
            for s in range(subs):
                def one(chunk, carry):
                    piece = pl.ds(pl.multiple_of(chunk * 64, 64), 64)
                    high, low = split(source[s, piece, :])
                    high_ref[s, piece, :] = high
                    low_ref[s, piece, :] = low
                    return carry
                lax.fori_loop(0, interior_size // 64, one, 0)

    def multiply(value, high_ref, low_ref, s):
        high, low = split(value)
        stacked = jnp.concatenate([high, low], axis=0)
        pieces = []
        for chunk in range(interior_size // 256):
            piece = slice(chunk * 256, (chunk + 1) * 256)
            product = dot_rows(stacked, high_ref[s, piece, :])
            pieces.append(product[0:CASES] + product[CASES:2 * CASES] + dot_rows(high, low_ref[s, piece, :]))
        return jnp.concatenate(pieces, axis=1)

    def picked(fetch, s):
        pieces = []
        for pair in range(adj.shape[1] // 2):
            halves = []
            for side in range(2):
                slot_id = 2 * pair + side
                both = doubled(fetch, adj[s, slot_id])
                halves.append(jnp.where(jnp.full((CASES, LANES), live[s]) > slot_id, both, 0.0))
            pieces.append(jnp.where(upper == 0, halves[0], halves[1]))
        return jnp.concatenate(pieces, axis=1)

    def recover(fetch, s):
        return multiply(multiply(picked(fetch, s), coup_h, coup_l, s), inv_h, inv_l, s)

    own = (members + m) * pairs
    win_load[pl.ds(own, pairs)] = load_ref[...]
    send_own(0)
    prepare_values()
    forward_line(0)
    forward_side(0)
    prepare_recovery()
    for s in range(subs):
        base[0, s] = multiply(iload_ref[s], inv_h, inv_l, s)
    await_regions(0)

    def fetch_load(tile):
        return win_load[tile]

    load = load_ref[...]
    image = apply_schur(fetch_load)
    win_image[pl.ds(own, pairs)] = image
    sum_start(0, [jnp.sum(load * load, axis=0), jnp.sum(load * image, axis=0)])
    send_own(1)
    forward_line(1)
    sum_middle(0)
    forward_side(1)
    for s in range(subs):
        base[1, s] = recover(fetch_load, s)
    norm, curve = sum_end(0, 2)
    step = norm / curve
    await_regions(1)

    def fetch_residual(tile):
        return win_load[tile] - step * win_image[tile]

    second = apply_schur(fetch_residual)
    residual = load - step * image
    second_ref[...] = second
    sum_start(1, [jnp.sum(residual * residual, axis=0), jnp.sum(residual * second, axis=0),
                  jnp.sum(residual * image + load * second, axis=0)])
    sum_middle(1)
    for s in range(subs):
        base[2, s] = recover(fetch_residual, s)
    norm_next, square, cross = sum_end(1, 3)
    ratio = norm_next / norm
    step_two = norm_next / (square + ratio * (cross + ratio * curve))
    along = step + step_two * ratio
    result_ref[...] = along * load + step_two * residual
    final_ref[...] = residual - step_two * (second_ref[...] + ratio * image)
    for s in range(subs):
        interior_ref[s] = base[0, s] - along * base[1, s] - step_two * base[2, s]
    finish_sends(0)
    finish_sends(1)


def body(interface_load, schur_values, schur_columns, coupling, layer_inverse, interior_load, adjacency, live_counts):
    block_rows = interface_load.shape[0]
    slots = schur_columns.shape[1]
    members = lax.axis_size("member")
    regions = lax.axis_size("region")
    outer = 4 if members % 4 == 0 else members
    inner = members // outer
    pairs = block_rows // 2
    groups = schur_values.shape[2] // LANES
    subs, size = interior_load.shape[0], interior_load.shape[2]
    packed = interface_load.reshape(pairs, 2, CASES, NB).transpose(0, 2, 1, 3).reshape(pairs, CASES, LANES)
    smem = pl.BlockSpec(memory_space=pltpu.SMEM)
    vmem = pl.BlockSpec(memory_space=pltpu.VMEM)
    anywhere = pl.BlockSpec(memory_space=pl.ANY)
    dma = pltpu.SemaphoreType.DMA
    result, final, interior = pl.pallas_call(
        functools.partial(fused_kernel, regions, outer, inner),
        out_shape=(
            jax.ShapeDtypeStruct(packed.shape, F32),
            jax.ShapeDtypeStruct(packed.shape, F32),
            jax.ShapeDtypeStruct(interior_load.shape, F32),
        ),
        in_specs=[smem, smem, smem, vmem, vmem, anywhere, anywhere, anywhere],
        out_specs=(vmem, vmem, vmem),
        scratch_shapes=[
            pltpu.VMEM((3 * members * pairs, CASES, LANES), F32),
            pltpu.VMEM((3 * members * pairs, CASES, LANES), F32),
            pltpu.VMEM(packed.shape, F32),
            pltpu.VMEM((block_rows, slots // 8, groups, 8, LANES), F32),
            pltpu.VMEM((block_rows, 2 * groups, slots * LANES), BF16),
            pltpu.VMEM((block_rows, 4 * CASES, slots * LANES), BF16),
            pltpu.VMEM((2, 2, pairs, CASES, 2 * groups), F32),
            pltpu.VMEM(coupling.shape, F32),
            pltpu.VMEM(coupling.shape, BF16),
            pltpu.VMEM(coupling.shape, BF16),
            pltpu.VMEM(layer_inverse.shape, F32),
            pltpu.VMEM(layer_inverse.shape, BF16),
            pltpu.VMEM(layer_inverse.shape, BF16),
            pltpu.VMEM((3, subs, CASES, size), F32),
            pltpu.VMEM((2, members, CASES, LANES), F32),
            pltpu.VMEM((2, regions, CASES, LANES), F32),
            dma((slots // 8, groups)),
            dma((2,)),
            dma((2, 3, outer, inner)),
            dma((2, outer)),
            dma((2, outer, inner)),
            dma((2, 2, outer, inner)),
            dma((2, members)),
            dma((2, members)),
            dma((2, regions)),
            dma((2, regions)),
        ],
        compiler_params=pltpu.CompilerParams(
            collective_id=0, has_side_effects=True, vmem_limit_bytes=56 * 2**20
        ),
    )(schur_columns, adjacency, live_counts, packed, interior_load, schur_values, coupling, layer_inverse)

    def unpack(value):
        return value.reshape(pairs, CASES, 2, NB).transpose(0, 2, 1, 3).reshape(block_rows, CASES * NB)

    return (unpack(result), unpack(final), interior)


def solution(mesh):
    in_specs = (
        P(("region", "member"), None),
        P(("region", "member"), None, None),
        P(("region", "member"), None),
        P(("region", "member"), None, None),
        P(("region", "member"), None, None),
        P(("region", "member"), None, None),
        P(("region", "member"), None),
        P(("region", "member")),
    )
    out_specs = (
        P(("region", "member"), None),
        P(("region", "member"), None),
        P(("region", "member"), None, None),
    )
    return jax.shard_map(body, mesh=mesh, in_specs=in_specs, out_specs=out_specs, check_vma=False)
```

```python
import functools

import jax
import jax.numpy as jnp
from jax import lax
from jax.experimental import pallas as pl
from jax.experimental.pallas import tpu as pltpu
from jax.sharding import PartitionSpec as P

NB = 64
CASES = 16
LANES = 2 * NB
MESH = pl.DeviceIdType.MESH
F32 = jnp.float32
BF16 = jnp.bfloat16


def split(value):
    high = value.astype(BF16)
    return high, (value - high.astype(F32)).astype(BF16)


def dot_rows(left, right, precision=None):
    return lax.dot_general(left, right, (((1,), (1,)), ((), ())), precision=precision, preferred_element_type=F32)


def fused_kernel(regions, outer, inner, cols, adj, live, given_ref, iload_ref, values_hbm, coupling_hbm, inverse_hbm,
                 result_ref, final_ref, interior_ref,
                 win_load, win_image, load_ref, second_ref, tiles_ref, values_ref, xx, raw, coup, coup_h, coup_l, inv, inv_h, inv_l, base, parts, rows,
                 value_sem, big_sem, recv_sem, line_sem, side_sem, region_sem,
                 member_send, member_recv, row_send, row_recv):
    members = outer * inner
    windows = (win_load, win_image)
    block_rows = cols.shape[0]
    slots = cols.shape[1]
    pairs = block_rows // 2
    subs, interior_size = iload_ref.shape[0], iload_ref.shape[2]
    groups = values_hbm.shape[2] // LANES
    octets = slots // 8
    g = lax.axis_index("region")
    m = lax.axis_index("member")
    a = m // inner
    b = m % inner
    has_low = g > 0
    has_high = g < regions - 1
    barrier = pltpu.get_barrier_semaphore()
    lane = lax.broadcasted_iota(jnp.int32, (CASES, LANES), 1)
    upper = lane // NB

    def value_copy(octet, group):
        return pltpu.make_async_copy(
            values_hbm.at[:, pl.ds(octet * 8, 8), pl.ds(pl.multiple_of(group * LANES, LANES), LANES)],
            tiles_ref.at[:, octet, group], value_sem.at[octet, group])

    def greet(region, member):
        pl.semaphore_signal(barrier, inc=1, device_id=(region, member), device_id_type=MESH)

    for step in range(1, members):
        greet(g, lax.rem(m + step, members))
    for step in range(1, regions):
        greet(lax.rem(g + step, regions), m)

    for octet in range(octets):
        def start_values(group, carry):
            value_copy(octet, group).start()
            return carry
        lax.fori_loop(0, groups, start_values, 0)
    big = [pltpu.make_async_copy(coupling_hbm, coup, big_sem.at[0]),
           pltpu.make_async_copy(inverse_hbm, inv, big_sem.at[1])]
    for copy in big:
        copy.start()

    def remote(source, target, send, recv, region, member):
        return pltpu.make_async_remote_copy(
            src_ref=source, dst_ref=target, send_sem=send, recv_sem=recv,
            device_id=(region, member), device_id_type=MESH,
        )

    def slot(turn, rel, row, column):
        first = ((rel * outer + row) * inner + column) * pairs
        return windows[turn].at[pl.ds(first, pairs)]

    def line_copy(turn, step):
        here = slot(turn, 1, a, b)
        return remote(here, here, line_sem.at[turn, step], recv_sem.at[turn, 1, a, b],
                      g, lax.rem(a + step, outer) * inner + b)

    def side_copy(turn, row, step):
        here = slot(turn, 1, row, b)
        return remote(here, here, side_sem.at[turn, row, step], recv_sem.at[turn, 1, row, b],
                      g, a * inner + lax.rem(b + step, inner))

    def region_copy(turn, row, column, up):
        rel = 0 if up else 2
        return remote(slot(turn, 1, row, column), slot(turn, rel, row, column),
                      region_sem.at[turn, rel // 2, row, column],
                      recv_sem.at[turn, rel, row, column], g + 1 if up else g - 1, m)

    def spread_regions(turn, row, column):
        @pl.when(has_high)
        def _():
            region_copy(turn, row, column, True).start()

        @pl.when(has_low)
        def _():
            region_copy(turn, row, column, False).start()

    def await_slot(turn, rel, row, column):
        here = slot(turn, rel, row, column)
        remote(here, here, line_sem.at[turn, 0], recv_sem.at[turn, rel, row, column], g, m).wait_recv()

    def send_own(turn):
        for step in range(1, outer):
            line_copy(turn, step).start()
        for step in range(1, inner):
            side_copy(turn, a, step).start()
        spread_regions(turn, a, b)

    def forward_line(turn, step):
        row = lax.rem(a + outer - step, outer)
        await_slot(turn, 1, row, b)
        for side in range(1, inner):
            side_copy(turn, row, side).start()
        spread_regions(turn, row, b)

    def forward_side(turn, step):
        row = lax.rem(a + outer - step, outer)
        for side in range(1, inner):
            column = lax.rem(b + inner - side, inner)
            await_slot(turn, 1, row, column)
            spread_regions(turn, row, column)

    def forward_all(turn, work):
        work = list(work)
        count = 2 * outer - 1
        for place in range(count):
            if place % 2:
                forward_line(turn, (place + 1) // 2)
            else:
                forward_side(turn, place // 2)
            for item in work[place * len(work) // count:(place + 1) * len(work) // count]:
                item()

    def await_regions(turn):
        for row in range(outer):
            for column in range(inner):
                @pl.when(has_low)
                def _():
                    await_slot(turn, 0, row, column)

                @pl.when(has_high)
                def _():
                    await_slot(turn, 2, row, column)

    def finish_sends(turn):
        for step in range(1, outer):
            line_copy(turn, step).wait_send()
        for row in range(outer):
            for step in range(1, inner):
                side_copy(turn, row, step).wait_send()
            for column in range(inner):
                @pl.when(has_low)
                def _():
                    region_copy(turn, row, column, False).wait_send()

                @pl.when(has_high)
                def _():
                    region_copy(turn, row, column, True).wait_send()

    def member_copy(turn, step):
        here = parts.at[turn, m]
        return remote(here, here, member_send.at[turn, step], member_recv.at[turn, m], g, lax.rem(m + step, members))

    def row_copy(turn, step):
        here = rows.at[turn, g]
        return remote(here, here, row_send.at[turn, step], row_recv.at[turn, g], lax.rem(g + step, regions), m)

    def sum_start(turn, products):
        packed = jnp.zeros((CASES, LANES), F32)
        for place, product in enumerate(products):
            packed = jnp.where(lane == place, jnp.sum(product, axis=1, keepdims=True), packed)
        parts[turn, m] = packed
        for step in range(1, members):
            member_copy(turn, step).start()

    def sum_middle(turn):
        for step in range(1, members):
            other = lax.rem(m + step, members)
            here = parts.at[turn, other]
            remote(here, here, member_send.at[turn, 0], member_recv.at[turn, other], g, other).wait_recv()
        total = parts[turn, 0]
        for other in range(1, members):
            total = total + parts[turn, other]
        rows[turn, g] = total
        for step in range(1, regions):
            row_copy(turn, step).start()

    def sum_end(turn, count):
        for step in range(1, regions):
            other = lax.rem(g + step, regions)
            here = rows.at[turn, other]
            remote(here, here, row_send.at[turn, 0], row_recv.at[turn, other], other, m).wait_recv()
        total = rows[turn, 0]
        for other in range(1, regions):
            total = total + rows[turn, other]
        for step in range(1, members):
            member_copy(turn, step).wait_send()
        for step in range(1, regions):
            row_copy(turn, step).wait_send()
        return [jnp.sum(jnp.where(lane == place, total, 0.0), axis=1, keepdims=True) for place in range(count)]

    first_id = (g - 1) * (block_rows * members)

    def prepare_values(first, count):
        flat = tiles_ref.reshape(block_rows * octets * groups * 8, LANES)

        def one(i, carry):
            for k in range(slots):
                start = (i * octets + k // 8) * (groups * 8) + k % 8
                high, low = split(flat[pl.ds(start, groups, stride=8), :])
                values_ref[i, 0:groups, k * LANES:(k + 1) * LANES] = high
                values_ref[i, groups:2 * groups, k * LANES:(k + 1) * LANES] = low
            return carry
        lax.fori_loop(first, first + count, one, 0)

    def await_values():
        for octet in range(octets):
            def wait_values(group, carry):
                value_copy(octet, group).wait()
                return carry
            lax.fori_loop(0, groups, wait_values, 0)

    def doubled(fetch, block):
        local = jnp.clip(block - first_id, 0, 3 * members * block_rows - 1)
        tile = fetch(lax.shift_right_logical(local, 1))
        kept = jnp.where(upper == lax.bitwise_and(local, 1), tile, 0.0)
        return kept + pltpu.roll(kept, NB, 1)

    def apply_schur(fetch):
        def four(u, carry):
            for j in range(4):
                i = 4 * u + j
                for k in range(slots):
                    both = doubled(fetch, cols[i, k])
                    place = slice(k * LANES, (k + 1) * LANES)
                    for p in range(2):
                        high, low = split(jnp.where(upper == p, both, 0.0))
                        xx[j, p * CASES:(p + 1) * CASES, place] = high
                        xx[j, (2 + p) * CASES:(3 + p) * CASES, place] = low
                product = dot_rows(xx[j], values_ref[i])
                product = product[0:2 * CASES] + product[2 * CASES:4 * CASES]
                for p in range(2):
                    raw[j % 2, p, 2 * u + j // 2] = product[p * CASES:(p + 1) * CASES]
            return carry
        lax.fori_loop(0, block_rows // 4, four, 0)
        lanes = 8 * groups
        place = lax.broadcasted_iota(jnp.int32, (LANES, lanes), 0)
        source = lax.broadcasted_iota(jnp.int32, (LANES, lanes), 1)
        part = source // (2 * groups)
        chosen = jnp.where(place == part // 2 * NB + 2 * (source % groups) + part % 2, 1.0, 0.0).astype(BF16)
        joined = jnp.concatenate(
            [raw[parity, p].reshape(pairs * CASES, 2 * groups) for parity in range(2) for p in range(2)], axis=1)
        high = joined.astype(BF16)
        rest = joined - high.astype(F32)
        middle, low = split(rest)
        total = dot_rows(high, chosen) + (dot_rows(middle, chosen) + dot_rows(low, chosen))
        return total.reshape(pairs, CASES, LANES)

    def prepare_recovery(source, high_ref, low_ref, s):
        def one(chunk, carry):
            piece = pl.ds(pl.multiple_of(chunk * 64, 64), 64)
            high, low = split(source[s, piece, :])
            high_ref[s, piece, :] = high
            low_ref[s, piece, :] = low
            return carry
        lax.fori_loop(0, interior_size // 64, one, 0)

    def multiply(value, high_ref, low_ref, s):
        high, low = split(value)
        stacked = jnp.concatenate([high, low], axis=0)
        pieces = []
        for chunk in range(interior_size // 256):
            piece = slice(chunk * 256, (chunk + 1) * 256)
            product = dot_rows(stacked, high_ref[s, piece, :])
            pieces.append(product[0:CASES] + product[CASES:2 * CASES] + dot_rows(high, low_ref[s, piece, :]))
        return jnp.concatenate(pieces, axis=1)

    def picked(fetch, s):
        pieces = []
        for pair in range(adj.shape[1] // 2):
            halves = []
            for side in range(2):
                slot_id = 2 * pair + side
                both = doubled(fetch, adj[s, slot_id])
                halves.append(jnp.where(jnp.full((CASES, LANES), live[s]) > slot_id, both, 0.0))
            pieces.append(jnp.where(upper == 0, halves[0], halves[1]))
        return jnp.concatenate(pieces, axis=1)

    def recover(fetch, s):
        return multiply(multiply(picked(fetch, s), coup_h, coup_l, s), inv_h, inv_l, s)

    own = (members + m) * pairs
    load_flat = load_ref.reshape(pairs * CASES, LANES)
    stage = second_ref.reshape(pairs * CASES, LANES)
    left = lax.broadcasted_iota(jnp.int32, (pairs, LANES), 1) < NB
    for pair in range(CASES // 2):
        stage[pair * block_rows:(pair + 1) * block_rows] = given_ref[:, pair * LANES:(pair + 1) * LANES]
    for pair in range(CASES // 2):
        even = stage[pl.ds(pair * block_rows, pairs, stride=2), :]
        odd = stage[pl.ds(pair * block_rows + 1, pairs, stride=2), :]
        load_flat[pl.ds(2 * pair, pairs, stride=CASES), :] = jnp.where(left, even, pltpu.roll(odd, NB, 1))
        load_flat[pl.ds(2 * pair + 1, pairs, stride=CASES), :] = jnp.where(left, pltpu.roll(even, NB, 1), odd)
    win_load[pl.ds(own, pairs)] = load_ref[...]
    pl.semaphore_wait(barrier, members - 1 + regions - 1)
    send_own(0)
    await_values()
    quarter = block_rows // 4
    forward_all(0, [functools.partial(prepare_values, first, quarter) for first in range(0, block_rows, quarter)])
    for copy in big:
        copy.wait()
    for s in range(subs):
        prepare_recovery(coup, coup_h, coup_l, s)
    await_regions(0)

    def fetch_load(tile):
        return win_load[tile]

    load = load_ref[...]
    image = apply_schur(fetch_load)
    win_image[pl.ds(own, pairs)] = image
    sum_start(0, [jnp.sum(load * load, axis=0), jnp.sum(load * image, axis=0)])
    send_own(1)

    def base_load(s):
        base[0, s] = multiply(iload_ref[s], inv_h, inv_l, s)

    def base_first(s):
        base[1, s] = recover(fetch_load, s)

    work = [functools.partial(prepare_recovery, inv, inv_h, inv_l, s) for s in range(subs)]
    work += [functools.partial(item, s) for item in (base_load, base_first) for s in range(subs)]
    forward_all(1, work[:subs])
    sum_middle(0)
    for item in work[subs:]:
        item()
    norm, curve = sum_end(0, 2)
    step = norm / curve
    await_regions(1)

    def fetch_residual(tile):
        return win_load[tile] - step * win_image[tile]

    second = apply_schur(fetch_residual)
    residual = load - step * image
    second_ref[...] = second
    sum_start(1, [jnp.sum(residual * residual, axis=0), jnp.sum(residual * second, axis=0),
                  jnp.sum(residual * image + load * second, axis=0)])
    for s in range(subs):
        base[2, s] = recover(fetch_residual, s)
        if s == 0:
            sum_middle(1)
    norm_next, square, cross = sum_end(1, 3)
    ratio = norm_next / norm
    step_two = norm_next / (square + ratio * (cross + ratio * curve))
    along = step + step_two * ratio
    result_ref[...] = along * load + step_two * residual
    final_ref[...] = residual - step_two * (second_ref[...] + ratio * image)
    for s in range(subs):
        interior_ref[s] = base[0, s] - along * base[1, s] - step_two * base[2, s]
    finish_sends(0)
    finish_sends(1)


def unpack_kernel(result, final, interior, result_out, final_out, interior_out, stage):
    pairs = result.shape[0]
    block_rows = 2 * pairs
    left = lax.broadcasted_iota(jnp.int32, (pairs, LANES), 1) < NB
    for source, target in ((result, result_out), (final, final_out)):
        flat = source.reshape(pairs * CASES, LANES)
        for pair in range(CASES // 2):
            even = flat[pl.ds(2 * pair, pairs, stride=CASES), :]
            odd = flat[pl.ds(2 * pair + 1, pairs, stride=CASES), :]
            stage[pl.ds(pair * block_rows, pairs, stride=2), :] = jnp.where(left, even, pltpu.roll(odd, NB, 1))
            stage[pl.ds(pair * block_rows + 1, pairs, stride=2), :] = jnp.where(left, pltpu.roll(even, NB, 1), odd)
        for pair in range(CASES // 2):
            target[:, pair * LANES:(pair + 1) * LANES] = stage[pair * block_rows:(pair + 1) * block_rows]
    interior_out[...] = interior[...]


def body(interface_load, schur_values, schur_columns, coupling, layer_inverse, interior_load, adjacency, live_counts):
    block_rows = interface_load.shape[0]
    slots = schur_columns.shape[1]
    members = lax.axis_size("member")
    regions = lax.axis_size("region")
    outer = 4 if members % 4 == 0 else members
    inner = members // outer
    pairs = block_rows // 2
    groups = schur_values.shape[2] // LANES
    subs, size = interior_load.shape[0], interior_load.shape[2]
    packed = (pairs, CASES, LANES)
    smem = pl.BlockSpec(memory_space=pltpu.SMEM)
    vmem = pl.BlockSpec(memory_space=pltpu.VMEM)
    anywhere = pl.BlockSpec(memory_space=pl.ANY)
    dma = pltpu.SemaphoreType.DMA
    result, final, interior = pl.pallas_call(
        functools.partial(fused_kernel, regions, outer, inner),
        out_shape=(
            jax.ShapeDtypeStruct(packed, F32),
            jax.ShapeDtypeStruct(packed, F32),
            jax.ShapeDtypeStruct(interior_load.shape, F32),
        ),
        in_specs=[smem, smem, smem, vmem, vmem, anywhere, anywhere, anywhere],
        out_specs=(vmem, vmem, vmem),
        scratch_shapes=[
            pltpu.VMEM((3 * members * pairs, CASES, LANES), F32),
            pltpu.VMEM((3 * members * pairs, CASES, LANES), F32),
            pltpu.VMEM(packed, F32),
            pltpu.VMEM(packed, F32),
            pltpu.VMEM((block_rows, slots // 8, groups, 8, LANES), F32),
            pltpu.VMEM((block_rows, 2 * groups, slots * LANES), BF16),
            pltpu.VMEM((4, 4 * CASES, slots * LANES), BF16),
            pltpu.VMEM((2, 2, pairs, CASES, 2 * groups), F32),
            pltpu.VMEM(coupling.shape, F32),
            pltpu.VMEM(coupling.shape, BF16),
            pltpu.VMEM(coupling.shape, BF16),
            pltpu.VMEM(layer_inverse.shape, F32),
            pltpu.VMEM(layer_inverse.shape, BF16),
            pltpu.VMEM(layer_inverse.shape, BF16),
            pltpu.VMEM((3, subs, CASES, size), F32),
            pltpu.VMEM((2, members, CASES, LANES), F32),
            pltpu.VMEM((2, regions, CASES, LANES), F32),
            dma((slots // 8, groups)),
            dma((2,)),
            dma((2, 3, outer, inner)),
            dma((2, outer)),
            dma((2, outer, inner)),
            dma((2, 2, outer, inner)),
            dma((2, members)),
            dma((2, members)),
            dma((2, regions)),
            dma((2, regions)),
        ],
        compiler_params=pltpu.CompilerParams(
            collective_id=0, has_side_effects=True, vmem_limit_bytes=56 * 2**20
        ),
    )(schur_columns, adjacency, live_counts, interface_load, interior_load, schur_values, coupling, layer_inverse)

    return pl.pallas_call(
        unpack_kernel,
        out_shape=(
            jax.ShapeDtypeStruct(interface_load.shape, F32),
            jax.ShapeDtypeStruct(interface_load.shape, F32),
            jax.ShapeDtypeStruct(interior_load.shape, F32),
        ),
        in_specs=[vmem] * 3,
        out_specs=(vmem,) * 3,
        scratch_shapes=[pltpu.VMEM((pairs * CASES, LANES), F32)],
    )(result, final, interior)


def solution(mesh):
    in_specs = (
        P(("region", "member"), None),
        P(("region", "member"), None, None),
        P(("region", "member"), None),
        P(("region", "member"), None, None),
        P(("region", "member"), None, None),
        P(("region", "member"), None, None),
        P(("region", "member"), None),
        P(("region", "member")),
    )
    out_specs = (
        P(("region", "member"), None),
        P(("region", "member"), None),
        P(("region", "member"), None, None),
    )
    return jax.shard_map(body, mesh=mesh, in_specs=in_specs, out_specs=out_specs, check_vma=False)
```

```python
import functools

import jax
import jax.numpy as jnp
from jax import lax
from jax.experimental import pallas as pl
from jax.experimental.pallas import tpu as pltpu
from jax.sharding import PartitionSpec as P

NB = 64
CASES = 16
LANES = 2 * NB
MESH = pl.DeviceIdType.MESH
F32 = jnp.float32
BF16 = jnp.bfloat16


def split(value):
    high = value.astype(BF16)
    return high, (value - high.astype(F32)).astype(BF16)


def dot_rows(left, right, precision=None):
    return lax.dot_general(left, right, (((1,), (1,)), ((), ())), precision=precision, preferred_element_type=F32)


def fused_kernel(regions, outer, inner, cols, adj, live, given_ref, iload_ref, values_hbm, coupling_hbm, inverse_hbm,
                 result_ref, final_ref, interior_ref,
                 win_load, win_image, load_ref, second_ref, tiles_ref, values_ref, xx, raw, coup, coup_h, coup_l, inv, inv_h, inv_l, base, parts, rows,
                 value_sem, big_sem, recv_sem, line_sem, side_sem, region_sem,
                 member_send, member_recv, row_send, row_recv):
    members = outer * inner
    windows = (win_load, win_image)
    block_rows = cols.shape[0]
    slots = cols.shape[1]
    pairs = block_rows // 2
    subs, interior_size = iload_ref.shape[0], iload_ref.shape[2]
    groups = values_hbm.shape[2] // LANES
    octets = slots // 8
    g = lax.axis_index("region")
    m = lax.axis_index("member")
    a = m // inner
    b = m % inner
    has_low = g > 0
    has_high = g < regions - 1
    barrier = pltpu.get_barrier_semaphore()
    lane = lax.broadcasted_iota(jnp.int32, (CASES, LANES), 1)
    upper = lane // NB

    def value_copy(octet, group):
        return pltpu.make_async_copy(
            values_hbm.at[:, pl.ds(octet * 8, 8), pl.ds(pl.multiple_of(group * LANES, LANES), LANES)],
            tiles_ref.at[:, octet, group], value_sem.at[octet, group])

    def greet(region, member):
        pl.semaphore_signal(barrier, inc=1, device_id=(region, member), device_id_type=MESH)

    for step in range(1, members):
        greet(g, lax.rem(m + step, members))
    for step in range(1, regions):
        greet(lax.rem(g + step, regions), m)

    for octet in range(octets):
        def start_values(group, carry):
            value_copy(octet, group).start()
            return carry
        lax.fori_loop(0, groups, start_values, 0)
    big = [pltpu.make_async_copy(coupling_hbm, coup, big_sem.at[0]),
           pltpu.make_async_copy(inverse_hbm, inv, big_sem.at[1])]
    for copy in big:
        copy.start()

    def remote(source, target, send, recv, region, member):
        return pltpu.make_async_remote_copy(
            src_ref=source, dst_ref=target, send_sem=send, recv_sem=recv,
            device_id=(region, member), device_id_type=MESH,
        )

    def slot(turn, rel, row, column):
        first = ((rel * outer + row) * inner + column) * pairs
        return windows[turn].at[pl.ds(first, pairs)]

    def line_copy(turn, step):
        here = slot(turn, 1, a, b)
        return remote(here, here, line_sem.at[turn, step], recv_sem.at[turn, 1, a, b],
                      g, lax.rem(a + step, outer) * inner + b)

    def side_copy(turn, row, step):
        here = slot(turn, 1, row, b)
        return remote(here, here, side_sem.at[turn, row, step], recv_sem.at[turn, 1, row, b],
                      g, a * inner + lax.rem(b + step, inner))

    def region_copy(turn, row, column, up):
        rel = 0 if up else 2
        return remote(slot(turn, 1, row, column), slot(turn, rel, row, column),
                      region_sem.at[turn, rel // 2, row, column],
                      recv_sem.at[turn, rel, row, column], g + 1 if up else g - 1, m)

    def spread_regions(turn, row, column):
        @pl.when(has_high)
        def _():
            region_copy(turn, row, column, True).start()

        @pl.when(has_low)
        def _():
            region_copy(turn, row, column, False).start()

    def await_slot(turn, rel, row, column):
        here = slot(turn, rel, row, column)
        remote(here, here, line_sem.at[turn, 0], recv_sem.at[turn, rel, row, column], g, m).wait_recv()

    def send_own(turn):
        for step in range(1, outer):
            line_copy(turn, step).start()
        for step in range(1, inner):
            side_copy(turn, a, step).start()
        spread_regions(turn, a, b)

    def forward_line(turn, step):
        row = lax.rem(a + outer - step, outer)
        await_slot(turn, 1, row, b)
        for side in range(1, inner):
            side_copy(turn, row, side).start()
        spread_regions(turn, row, b)

    def forward_side(turn, step):
        row = lax.rem(a + outer - step, outer)
        for side in range(1, inner):
            column = lax.rem(b + inner - side, inner)
            await_slot(turn, 1, row, column)
            spread_regions(turn, row, column)

    def forward_all(turn, work):
        work = list(work)
        count = 2 * outer - 1
        for place in range(count):
            if place % 2:
                forward_line(turn, (place + 1) // 2)
            else:
                forward_side(turn, place // 2)
            for item in work[place * len(work) // count:(place + 1) * len(work) // count]:
                item()

    def await_regions(turn):
        for row in range(outer):
            for column in range(inner):
                @pl.when(has_low)
                def _():
                    await_slot(turn, 0, row, column)

                @pl.when(has_high)
                def _():
                    await_slot(turn, 2, row, column)

    def finish_sends(turn):
        for step in range(1, outer):
            line_copy(turn, step).wait_send()
        for row in range(outer):
            for step in range(1, inner):
                side_copy(turn, row, step).wait_send()
            for column in range(inner):
                @pl.when(has_low)
                def _():
                    region_copy(turn, row, column, False).wait_send()

                @pl.when(has_high)
                def _():
                    region_copy(turn, row, column, True).wait_send()

    def member_copy(turn, step):
        here = parts.at[turn, m]
        return remote(here, here, member_send.at[turn, step], member_recv.at[turn, m], g, lax.rem(m + step, members))

    def row_copy(turn, step):
        here = rows.at[turn, g]
        return remote(here, here, row_send.at[turn, step], row_recv.at[turn, g], lax.rem(g + step, regions), m)

    def sum_start(turn, products):
        packed = jnp.zeros((CASES, LANES), F32)
        for place, product in enumerate(products):
            packed = jnp.where(lane == place, jnp.sum(product, axis=1, keepdims=True), packed)
        parts[turn, m] = packed
        for step in range(1, members):
            member_copy(turn, step).start()

    def sum_middle(turn):
        for step in range(1, members):
            other = lax.rem(m + step, members)
            here = parts.at[turn, other]
            remote(here, here, member_send.at[turn, 0], member_recv.at[turn, other], g, other).wait_recv()
        total = parts[turn, 0]
        for other in range(1, members):
            total = total + parts[turn, other]
        rows[turn, g] = total
        for step in range(1, regions):
            row_copy(turn, step).start()

    def sum_end(turn, count):
        for step in range(1, regions):
            other = lax.rem(g + step, regions)
            here = rows.at[turn, other]
            remote(here, here, row_send.at[turn, 0], row_recv.at[turn, other], other, m).wait_recv()
        total = rows[turn, 0]
        for other in range(1, regions):
            total = total + rows[turn, other]
        for step in range(1, members):
            member_copy(turn, step).wait_send()
        for step in range(1, regions):
            row_copy(turn, step).wait_send()
        return [jnp.sum(jnp.where(lane == place, total, 0.0), axis=1, keepdims=True) for place in range(count)]

    first_id = (g - 1) * (block_rows * members)

    def prepare_values(first, count):
        flat = tiles_ref.reshape(block_rows * octets * groups * 8, LANES)
        wide = lax.broadcasted_iota(jnp.int32, (groups, LANES), 1) // NB

        def one(i, carry):
            for k in range(0, slots, 2):
                start = (i * octets + k // 8) * (groups * 8) + k % 8
                first_slot = flat[pl.ds(start, groups, stride=8), :]
                second_slot = flat[pl.ds(start + 1, groups, stride=8), :]
                place = slice(k // 2 * LANES, (k // 2 + 1) * LANES)
                for p, joined in enumerate((jnp.where(wide == 0, first_slot, pltpu.roll(second_slot, NB, 1)),
                                            jnp.where(wide == 0, pltpu.roll(first_slot, NB, 1), second_slot))):
                    high, low = split(joined)
                    values_ref[i, p * groups:(p + 1) * groups, place] = high
                    values_ref[i, (2 + p) * groups:(3 + p) * groups, place] = low
            return carry
        lax.fori_loop(first, first + count, one, 0)

    def await_values():
        for octet in range(octets):
            def wait_values(group, carry):
                value_copy(octet, group).wait()
                return carry
            lax.fori_loop(0, groups, wait_values, 0)

    def doubled(fetch, block):
        local = jnp.clip(block - first_id, 0, 3 * members * block_rows - 1)
        tile = fetch(lax.shift_right_logical(local, 1))
        kept = jnp.where(upper == lax.bitwise_and(local, 1), tile, 0.0)
        return kept + pltpu.roll(kept, NB, 1)

    def apply_schur(fetch):
        def four(u, carry):
            for j in range(4):
                i = 4 * u + j
                for k in range(0, slots, 2):
                    place = slice(k // 2 * LANES, (k // 2 + 1) * LANES)
                    high, low = split(jnp.where(upper == 0, doubled(fetch, cols[i, k]), doubled(fetch, cols[i, k + 1])))
                    xx[j, 0:CASES, place] = high
                    xx[j, CASES:2 * CASES, place] = low
                product = dot_rows(xx[j], values_ref[i])
                raw[j % 2, 2 * u + j // 2] = product[0:CASES] + product[CASES:2 * CASES]
            return carry
        lax.fori_loop(0, block_rows // 4, four, 0)
        place = lax.broadcasted_iota(jnp.int32, (LANES, 8 * groups), 0)
        source = lax.broadcasted_iota(jnp.int32, (LANES, 8 * groups), 1)
        target = source // (4 * groups) * NB + 2 * (source % groups) + source // groups % 2
        chosen = jnp.where(place == target, 1.0, 0.0).astype(BF16)
        joined = jnp.concatenate([raw[parity].reshape(pairs * CASES, 4 * groups) for parity in range(2)], axis=1)
        high = joined.astype(BF16)
        rest = joined - high.astype(F32)
        middle, low = split(rest)
        total = dot_rows(high, chosen) + (dot_rows(middle, chosen) + dot_rows(low, chosen))
        return total.reshape(pairs, CASES, LANES)

    def prepare_recovery(source, high_ref, low_ref, s):
        def one(chunk, carry):
            piece = pl.ds(pl.multiple_of(chunk * 64, 64), 64)
            high, low = split(source[s, piece, :])
            high_ref[s, piece, :] = high
            low_ref[s, piece, :] = low
            return carry
        lax.fori_loop(0, interior_size // 64, one, 0)

    def multiply(values, high_ref, low_ref, s):
        parted = [split(value) for value in values]
        count = len(values) * CASES
        highs = jnp.concatenate([high for high, _ in parted], axis=0)
        stacked = jnp.concatenate([highs] + [low for _, low in parted], axis=0)
        pieces = []
        for chunk in range(interior_size // 256):
            piece = slice(chunk * 256, (chunk + 1) * 256)
            product = dot_rows(stacked, high_ref[s, piece, :])
            pieces.append(product[0:count] + product[count:2 * count] + dot_rows(highs, low_ref[s, piece, :]))
        return jnp.concatenate(pieces, axis=1)

    def picked(fetch, s):
        pieces = []
        for pair in range(adj.shape[1] // 2):
            halves = []
            for side in range(2):
                slot_id = 2 * pair + side
                both = doubled(fetch, adj[s, slot_id])
                halves.append(jnp.where(jnp.full((CASES, LANES), live[s]) > slot_id, both, 0.0))
            pieces.append(jnp.where(upper == 0, halves[0], halves[1]))
        return jnp.concatenate(pieces, axis=1)

    def coupled(fetch, s):
        return multiply([picked(fetch, s)], coup_h, coup_l, s)

    own = (members + m) * pairs
    load_flat = load_ref.reshape(pairs * CASES, LANES)
    stage = second_ref.reshape(pairs * CASES, LANES)
    left = lax.broadcasted_iota(jnp.int32, (pairs, LANES), 1) < NB
    for pair in range(CASES // 2):
        stage[pair * block_rows:(pair + 1) * block_rows] = given_ref[:, pair * LANES:(pair + 1) * LANES]
    for pair in range(CASES // 2):
        even = stage[pl.ds(pair * block_rows, pairs, stride=2), :]
        odd = stage[pl.ds(pair * block_rows + 1, pairs, stride=2), :]
        load_flat[pl.ds(2 * pair, pairs, stride=CASES), :] = jnp.where(left, even, pltpu.roll(odd, NB, 1))
        load_flat[pl.ds(2 * pair + 1, pairs, stride=CASES), :] = jnp.where(left, pltpu.roll(even, NB, 1), odd)
    win_load[pl.ds(own, pairs)] = load_ref[...]
    pl.semaphore_wait(barrier, members - 1 + regions - 1)
    send_own(0)
    await_values()
    quarter = block_rows // 4
    forward_all(0, [functools.partial(prepare_values, first, quarter) for first in range(0, block_rows, quarter)])
    for copy in big:
        copy.wait()
    for s in range(subs):
        prepare_recovery(coup, coup_h, coup_l, s)
    await_regions(0)

    def fetch_load(tile):
        return win_load[tile]

    load = load_ref[...]
    image = apply_schur(fetch_load)
    win_image[pl.ds(own, pairs)] = image
    sum_start(0, [jnp.sum(load * load, axis=0), jnp.sum(load * image, axis=0)])
    send_own(1)

    def known_parts(s):
        both = multiply([iload_ref[s], coupled(fetch_load, s)], inv_h, inv_l, s)
        base[0, s] = both[0:CASES]
        base[1, s] = both[CASES:2 * CASES]

    work = [functools.partial(prepare_recovery, inv, inv_h, inv_l, s) for s in range(subs)]
    work += [functools.partial(known_parts, s) for s in range(subs)]
    forward_all(1, work[:subs])
    sum_middle(0)
    for item in work[subs:]:
        item()
    norm, curve = sum_end(0, 2)
    step = norm / curve
    await_regions(1)

    def fetch_residual(tile):
        return win_load[tile] - step * win_image[tile]

    second = apply_schur(fetch_residual)
    residual = load - step * image
    second_ref[...] = second
    sum_start(1, [jnp.sum(residual * residual, axis=0), jnp.sum(residual * second, axis=0),
                  jnp.sum(residual * image + load * second, axis=0)])
    for s in range(subs):
        base[2, s] = multiply([coupled(fetch_residual, s)], inv_h, inv_l, s)
        if s == 0:
            sum_middle(1)
    norm_next, square, cross = sum_end(1, 3)
    ratio = norm_next / norm
    step_two = norm_next / (square + ratio * (cross + ratio * curve))
    along = step + step_two * ratio
    result_ref[...] = along * load + step_two * residual
    final_ref[...] = residual - step_two * (second_ref[...] + ratio * image)
    for s in range(subs):
        interior_ref[s] = base[0, s] - along * base[1, s] - step_two * base[2, s]
    finish_sends(0)
    finish_sends(1)


def unpack_kernel(result, final, interior, result_out, final_out, interior_out, stage):
    pairs = result.shape[0]
    block_rows = 2 * pairs
    left = lax.broadcasted_iota(jnp.int32, (pairs, LANES), 1) < NB
    for source, target in ((result, result_out), (final, final_out)):
        flat = source.reshape(pairs * CASES, LANES)
        for pair in range(CASES // 2):
            even = flat[pl.ds(2 * pair, pairs, stride=CASES), :]
            odd = flat[pl.ds(2 * pair + 1, pairs, stride=CASES), :]
            stage[pl.ds(pair * block_rows, pairs, stride=2), :] = jnp.where(left, even, pltpu.roll(odd, NB, 1))
            stage[pl.ds(pair * block_rows + 1, pairs, stride=2), :] = jnp.where(left, pltpu.roll(even, NB, 1), odd)
        for pair in range(CASES // 2):
            target[:, pair * LANES:(pair + 1) * LANES] = stage[pair * block_rows:(pair + 1) * block_rows]
    interior_out[...] = interior[...]


def body(interface_load, schur_values, schur_columns, coupling, layer_inverse, interior_load, adjacency, live_counts):
    block_rows = interface_load.shape[0]
    slots = schur_columns.shape[1]
    members = lax.axis_size("member")
    regions = lax.axis_size("region")
    outer = 4 if members % 4 == 0 else members
    inner = members // outer
    pairs = block_rows // 2
    groups = schur_values.shape[2] // LANES
    subs, size = interior_load.shape[0], interior_load.shape[2]
    packed = (pairs, CASES, LANES)
    smem = pl.BlockSpec(memory_space=pltpu.SMEM)
    vmem = pl.BlockSpec(memory_space=pltpu.VMEM)
    anywhere = pl.BlockSpec(memory_space=pl.ANY)
    dma = pltpu.SemaphoreType.DMA
    result, final, interior = pl.pallas_call(
        functools.partial(fused_kernel, regions, outer, inner),
        out_shape=(
            jax.ShapeDtypeStruct(packed, F32),
            jax.ShapeDtypeStruct(packed, F32),
            jax.ShapeDtypeStruct(interior_load.shape, F32),
        ),
        in_specs=[smem, smem, smem, vmem, vmem, anywhere, anywhere, anywhere],
        out_specs=(vmem, vmem, vmem),
        scratch_shapes=[
            pltpu.VMEM((3 * members * pairs, CASES, LANES), F32),
            pltpu.VMEM((3 * members * pairs, CASES, LANES), F32),
            pltpu.VMEM(packed, F32),
            pltpu.VMEM(packed, F32),
            pltpu.VMEM((block_rows, slots // 8, groups, 8, LANES), F32),
            pltpu.VMEM((block_rows, 4 * groups, slots * NB), BF16),
            pltpu.VMEM((4, 2 * CASES, slots * NB), BF16),
            pltpu.VMEM((2, pairs, CASES, 4 * groups), F32),
            pltpu.VMEM(coupling.shape, F32),
            pltpu.VMEM(coupling.shape, BF16),
            pltpu.VMEM(coupling.shape, BF16),
            pltpu.VMEM(layer_inverse.shape, F32),
            pltpu.VMEM(layer_inverse.shape, BF16),
            pltpu.VMEM(layer_inverse.shape, BF16),
            pltpu.VMEM((3, subs, CASES, size), F32),
            pltpu.VMEM((2, members, CASES, LANES), F32),
            pltpu.VMEM((2, regions, CASES, LANES), F32),
            dma((slots // 8, groups)),
            dma((2,)),
            dma((2, 3, outer, inner)),
            dma((2, outer)),
            dma((2, outer, inner)),
            dma((2, 2, outer, inner)),
            dma((2, members)),
            dma((2, members)),
            dma((2, regions)),
            dma((2, regions)),
        ],
        compiler_params=pltpu.CompilerParams(
            collective_id=0, has_side_effects=True, vmem_limit_bytes=56 * 2**20
        ),
    )(schur_columns, adjacency, live_counts, interface_load, interior_load, schur_values, coupling, layer_inverse)

    return pl.pallas_call(
        unpack_kernel,
        out_shape=(
            jax.ShapeDtypeStruct(interface_load.shape, F32),
            jax.ShapeDtypeStruct(interface_load.shape, F32),
            jax.ShapeDtypeStruct(interior_load.shape, F32),
        ),
        in_specs=[vmem] * 3,
        out_specs=(vmem,) * 3,
        scratch_shapes=[pltpu.VMEM((pairs * CASES, LANES), F32)],
    )(result, final, interior)


def solution(mesh):
    in_specs = (
        P(("region", "member"), None),
        P(("region", "member"), None, None),
        P(("region", "member"), None),
        P(("region", "member"), None, None),
        P(("region", "member"), None, None),
        P(("region", "member"), None, None),
        P(("region", "member"), None),
        P(("region", "member")),
    )
    out_specs = (
        P(("region", "member"), None),
        P(("region", "member"), None),
        P(("region", "member"), None, None),
    )
    return jax.shard_map(body, mesh=mesh, in_specs=in_specs, out_specs=out_specs, check_vma=False)
```

```python
import functools

import jax
import jax.numpy as jnp
from jax import lax
from jax.experimental import pallas as pl
from jax.experimental.pallas import tpu as pltpu
from jax.sharding import PartitionSpec as P

NB = 64
CASES = 16
LANES = 2 * NB
MESH = pl.DeviceIdType.MESH
F32 = jnp.float32
BF16 = jnp.bfloat16


def split(value):
    high = value.astype(BF16)
    return high, (value - high.astype(F32)).astype(BF16)


def dot_rows(left, right, precision=None):
    return lax.dot_general(left, right, (((1,), (1,)), ((), ())), precision=precision, preferred_element_type=F32)


def fused_kernel(regions, outer, inner, cols, adj, live, given_ref, iload_ref, values_hbm, coupling_hbm, inverse_hbm,
                 result_ref, final_ref, interior_ref,
                 win_load, win_image, load_ref, second_ref, tiles_ref, values_ref, xx, raw, coup, coup_h, coup_l, inv, inv_h, inv_l, base, parts, rows,
                 value_sem, big_sem, recv_sem, line_sem, side_sem, region_sem,
                 member_send, member_recv, row_send, row_recv):
    members = outer * inner
    windows = (win_load, win_image)
    block_rows = cols.shape[0]
    slots = cols.shape[1]
    pairs = block_rows // 2
    subs, interior_size = iload_ref.shape[0], iload_ref.shape[2]
    groups = values_hbm.shape[2] // LANES
    octets = slots // 8
    g = lax.axis_index("region")
    m = lax.axis_index("member")
    a = m // inner
    b = m % inner
    has_low = g > 0
    has_high = g < regions - 1
    barrier = pltpu.get_barrier_semaphore()
    lane = lax.broadcasted_iota(jnp.int32, (CASES, LANES), 1)
    upper = lane // NB

    def value_copy(octet, group):
        return pltpu.make_async_copy(
            values_hbm.at[:, pl.ds(octet * 8, 8), pl.ds(pl.multiple_of(group * LANES, LANES), LANES)],
            tiles_ref.at[:, octet, group], value_sem.at[octet, group])

    def greet(region, member):
        pl.semaphore_signal(barrier, inc=1, device_id=(region, member), device_id_type=MESH)

    for step in range(1, members):
        greet(g, lax.rem(m + step, members))
    for step in range(1, regions):
        greet(lax.rem(g + step, regions), m)

    for octet in range(octets):
        def start_values(group, carry):
            value_copy(octet, group).start()
            return carry
        lax.fori_loop(0, groups, start_values, 0)
    big = [pltpu.make_async_copy(coupling_hbm, coup, big_sem.at[0]),
           pltpu.make_async_copy(inverse_hbm, inv, big_sem.at[1])]
    def remote(source, target, send, recv, region, member):
        return pltpu.make_async_remote_copy(
            src_ref=source, dst_ref=target, send_sem=send, recv_sem=recv,
            device_id=(region, member), device_id_type=MESH,
        )

    def slot(turn, rel, row, column):
        first = ((rel * outer + row) * inner + column) * pairs
        return windows[turn].at[pl.ds(first, pairs)]

    def line_copy(turn, step):
        here = slot(turn, 1, a, b)
        return remote(here, here, line_sem.at[turn, step], recv_sem.at[turn, 1, a, b],
                      g, lax.rem(a + step, outer) * inner + b)

    def side_copy(turn, row, step):
        here = slot(turn, 1, row, b)
        return remote(here, here, side_sem.at[turn, row, step], recv_sem.at[turn, 1, row, b],
                      g, a * inner + lax.rem(b + step, inner))

    def region_copy(turn, row, column, up):
        rel = 0 if up else 2
        return remote(slot(turn, 1, row, column), slot(turn, rel, row, column),
                      region_sem.at[turn, rel // 2, row, column],
                      recv_sem.at[turn, rel, row, column], g + 1 if up else g - 1, m)

    def spread_regions(turn, row, column):
        @pl.when(has_high)
        def _():
            region_copy(turn, row, column, True).start()

        @pl.when(has_low)
        def _():
            region_copy(turn, row, column, False).start()

    def await_slot(turn, rel, row, column):
        here = slot(turn, rel, row, column)
        remote(here, here, line_sem.at[turn, 0], recv_sem.at[turn, rel, row, column], g, m).wait_recv()

    def send_own(turn):
        for step in range(1, outer):
            line_copy(turn, step).start()
        for step in range(1, inner):
            side_copy(turn, a, step).start()
        spread_regions(turn, a, b)

    def forward_line(turn, step):
        row = lax.rem(a + outer - step, outer)
        await_slot(turn, 1, row, b)
        for side in range(1, inner):
            side_copy(turn, row, side).start()
        spread_regions(turn, row, b)

    def forward_side(turn, step):
        row = lax.rem(a + outer - step, outer)
        for side in range(1, inner):
            column = lax.rem(b + inner - side, inner)
            await_slot(turn, 1, row, column)
            spread_regions(turn, row, column)

    def forward_all(turn, work, skip):
        work = list(work)
        count = 2 * outer - 1
        for place in range(count):
            if place % 2:
                forward_line(turn, (place + 1) // 2)
            else:
                forward_side(turn, place // 2)
            if place >= skip:
                first, after = ((place + more - skip) * len(work) // (count - skip) for more in range(2))
                for item in work[first:after]:
                    item()

    def await_regions(turn):
        for row in range(outer):
            for column in range(inner):
                @pl.when(has_low)
                def _():
                    await_slot(turn, 0, row, column)

                @pl.when(has_high)
                def _():
                    await_slot(turn, 2, row, column)

    def finish_sends(turn):
        for step in range(1, outer):
            line_copy(turn, step).wait_send()
        for row in range(outer):
            for step in range(1, inner):
                side_copy(turn, row, step).wait_send()
            for column in range(inner):
                @pl.when(has_low)
                def _():
                    region_copy(turn, row, column, False).wait_send()

                @pl.when(has_high)
                def _():
                    region_copy(turn, row, column, True).wait_send()

    def member_copy(turn, step):
        here = parts.at[turn, m]
        return remote(here, here, member_send.at[turn, step], member_recv.at[turn, m], g, lax.rem(m + step, members))

    def row_copy(turn, step):
        here = rows.at[turn, g]
        return remote(here, here, row_send.at[turn, step], row_recv.at[turn, g], lax.rem(g + step, regions), m)

    def sum_start(turn, products):
        packed = jnp.zeros((CASES, LANES), F32)
        for place, product in enumerate(products):
            packed = jnp.where(lane == place, jnp.sum(product, axis=1, keepdims=True), packed)
        parts[turn, m] = packed
        for step in range(1, members):
            member_copy(turn, step).start()

    def sum_middle(turn):
        for step in range(1, members):
            other = lax.rem(m + step, members)
            here = parts.at[turn, other]
            remote(here, here, member_send.at[turn, 0], member_recv.at[turn, other], g, other).wait_recv()
        total = parts[turn, 0]
        for other in range(1, members):
            total = total + parts[turn, other]
        rows[turn, g] = total
        for step in range(1, regions):
            row_copy(turn, step).start()

    def sum_end(turn, count):
        for step in range(1, regions):
            other = lax.rem(g + step, regions)
            here = rows.at[turn, other]
            remote(here, here, row_send.at[turn, 0], row_recv.at[turn, other], other, m).wait_recv()
        total = rows[turn, 0]
        for other in range(1, regions):
            total = total + rows[turn, other]
        for step in range(1, members):
            member_copy(turn, step).wait_send()
        for step in range(1, regions):
            row_copy(turn, step).wait_send()
        return [jnp.sum(jnp.where(lane == place, total, 0.0), axis=1, keepdims=True) for place in range(count)]

    first_id = (g - 1) * (block_rows * members)

    def prepare_values(first, count):
        flat = tiles_ref.reshape(block_rows * octets * groups * 8, LANES)
        wide = lax.broadcasted_iota(jnp.int32, (groups, LANES), 1) // NB

        def one(i, carry):
            for k in range(0, slots, 2):
                start = (i * octets + k // 8) * (groups * 8) + k % 8
                first_slot = flat[pl.ds(start, groups, stride=8), :]
                second_slot = flat[pl.ds(start + 1, groups, stride=8), :]
                place = slice(k // 2 * LANES, (k // 2 + 1) * LANES)
                for p, joined in enumerate((jnp.where(wide == 0, first_slot, pltpu.roll(second_slot, NB, 1)),
                                            jnp.where(wide == 0, pltpu.roll(first_slot, NB, 1), second_slot))):
                    high, low = split(joined)
                    values_ref[i, p * groups:(p + 1) * groups, place] = high
                    values_ref[i, (2 + p) * groups:(3 + p) * groups, place] = low
            return carry
        lax.fori_loop(first, first + count, one, 0)

    def await_values():
        for octet in range(octets):
            def wait_values(group, carry):
                value_copy(octet, group).wait()
                return carry
            lax.fori_loop(0, groups, wait_values, 0)

    def doubled(fetch, block):
        local = jnp.clip(block - first_id, 0, 3 * members * block_rows - 1)
        tile = fetch(lax.shift_right_logical(local, 1))
        kept = jnp.where(upper == lax.bitwise_and(local, 1), tile, 0.0)
        return kept + pltpu.roll(kept, NB, 1)

    def apply_schur(fetch):
        def four(u, carry):
            for j in range(4):
                i = 4 * u + j
                for k in range(0, slots, 2):
                    place = slice(k // 2 * LANES, (k // 2 + 1) * LANES)
                    high, low = split(jnp.where(upper == 0, doubled(fetch, cols[i, k]), doubled(fetch, cols[i, k + 1])))
                    xx[j, 0:CASES, place] = high
                    xx[j, CASES:2 * CASES, place] = low
                product = dot_rows(xx[j], values_ref[i])
                raw[j % 2, 2 * u + j // 2] = product[0:CASES] + product[CASES:2 * CASES]
            return carry
        lax.fori_loop(0, block_rows // 4, four, 0)
        place = lax.broadcasted_iota(jnp.int32, (LANES, 8 * groups), 0)
        source = lax.broadcasted_iota(jnp.int32, (LANES, 8 * groups), 1)
        target = source // (4 * groups) * NB + 2 * (source % groups) + source // groups % 2
        chosen = jnp.where(place == target, 1.0, 0.0).astype(BF16)
        joined = jnp.concatenate([raw[parity].reshape(pairs * CASES, 4 * groups) for parity in range(2)], axis=1)
        high = joined.astype(BF16)
        rest = joined - high.astype(F32)
        middle, low = split(rest)
        total = dot_rows(high, chosen) + (dot_rows(middle, chosen) + dot_rows(low, chosen))
        return total.reshape(pairs, CASES, LANES)

    def prepare_recovery(source, high_ref, low_ref, s, part):
        def one(chunk, carry):
            piece = pl.ds(pl.multiple_of(chunk * 64, 64), 64)
            high, low = split(source[s, piece, :])
            high_ref[s, piece, :] = high
            low_ref[s, piece, :] = low
            return carry
        portion = interior_size // 128
        lax.fori_loop(part * portion, (part + 1) * portion, one, 0)

    def multiply(values, high_ref, low_ref, s, chunks=None):
        parted = [split(value) for value in values]
        count = len(values) * CASES
        highs = jnp.concatenate([high for high, _ in parted], axis=0)
        stacked = jnp.concatenate([highs] + [low for _, low in parted], axis=0)
        pieces = []
        for chunk in chunks or range(interior_size // 256):
            piece = slice(chunk * 256, (chunk + 1) * 256)
            product = dot_rows(stacked, high_ref[s, piece, :])
            pieces.append(product[0:count] + product[count:2 * count] + dot_rows(highs, low_ref[s, piece, :]))
        return jnp.concatenate(pieces, axis=1)

    def picked(fetch, s):
        pieces = []
        for pair in range(adj.shape[1] // 2):
            halves = []
            for side in range(2):
                slot_id = 2 * pair + side
                both = doubled(fetch, adj[s, slot_id])
                halves.append(jnp.where(jnp.full((CASES, LANES), live[s]) > slot_id, both, 0.0))
            pieces.append(jnp.where(upper == 0, halves[0], halves[1]))
        return jnp.concatenate(pieces, axis=1)

    def coupled(fetch, s):
        return multiply([picked(fetch, s)], coup_h, coup_l, s)

    own = (members + m) * pairs
    load_flat = load_ref.reshape(pairs * CASES, LANES)
    stage = second_ref.reshape(pairs * CASES, LANES)
    left = lax.broadcasted_iota(jnp.int32, (pairs, LANES), 1) < NB
    for pair in range(CASES // 2):
        stage[pair * block_rows:(pair + 1) * block_rows] = given_ref[:, pair * LANES:(pair + 1) * LANES]
    for pair in range(CASES // 2):
        even = stage[pl.ds(pair * block_rows, pairs, stride=2), :]
        odd = stage[pl.ds(pair * block_rows + 1, pairs, stride=2), :]
        load_flat[pl.ds(2 * pair, pairs, stride=CASES), :] = jnp.where(left, even, pltpu.roll(odd, NB, 1))
        load_flat[pl.ds(2 * pair + 1, pairs, stride=CASES), :] = jnp.where(left, pltpu.roll(even, NB, 1), odd)
    win_load[pl.ds(own, pairs)] = load_ref[...]
    pl.semaphore_wait(barrier, members - 1 + regions - 1)
    send_own(0)

    def operands_here():
        await_values()
        for copy in big:
            copy.start()

    part_rows = block_rows // 8
    pieces = [functools.partial(prepare_values, first, part_rows) for first in range(0, block_rows, part_rows)]
    forward_all(0, [operands_here] + pieces, 2)
    await_regions(0)

    def fetch_load(tile):
        return win_load[tile]

    load = load_ref[...]
    image = apply_schur(fetch_load)
    win_image[pl.ds(own, pairs)] = image
    send_own(1)
    sum_start(0, [jnp.sum(load * load, axis=0), jnp.sum(load * image, axis=0)])

    def big_here():
        for copy in big:
            copy.wait()

    def couple_known(s):
        base[3, s] = coupled(fetch_load, s)

    def solve_known(s, chunk):
        both = multiply([iload_ref[s], base[3, s]], inv_h, inv_l, s, (chunk,))
        place = slice(chunk * 256, (chunk + 1) * 256)
        base[0, s, :, place] = both[0:CASES]
        base[1, s, :, place] = both[CASES:2 * CASES]

    work = [big_here]
    for source, high_ref, low_ref in ((coup, coup_h, coup_l), (inv, inv_h, inv_l)):
        work += [functools.partial(prepare_recovery, source, high_ref, low_ref, s, part)
                 for s in range(subs) for part in range(2)]
    work.insert(len(work) // 2, functools.partial(sum_middle, 0))
    work += [functools.partial(couple_known, s) for s in range(subs)]
    work += [functools.partial(solve_known, s, chunk) for s in range(subs) for chunk in range(interior_size // 256)]
    late = len(work) // 3
    forward_all(1, work[:-late], 0)
    for item in work[-late:]:
        item()
    norm, curve = sum_end(0, 2)
    step = norm / curve
    await_regions(1)

    def fetch_residual(tile):
        return win_load[tile] - step * win_image[tile]

    second = apply_schur(fetch_residual)
    residual = load - step * image
    second_ref[...] = second
    sum_start(1, [jnp.sum(residual * residual, axis=0), jnp.sum(residual * second, axis=0),
                  jnp.sum(residual * image + load * second, axis=0)])
    for s in range(subs):
        base[2, s] = multiply([coupled(fetch_residual, s)], inv_h, inv_l, s)
        if s == 0:
            sum_middle(1)
    norm_next, square, cross = sum_end(1, 3)
    ratio = norm_next / norm
    step_two = norm_next / (square + ratio * (cross + ratio * curve))
    along = step + step_two * ratio
    result_ref[...] = along * load + step_two * residual
    final_ref[...] = residual - step_two * (second_ref[...] + ratio * image)
    for s in range(subs):
        interior_ref[s] = base[0, s] - along * base[1, s] - step_two * base[2, s]
    finish_sends(0)
    finish_sends(1)


def unpack_kernel(result, final, interior, result_out, final_out, interior_out, stage):
    pairs = result.shape[0]
    block_rows = 2 * pairs
    left = lax.broadcasted_iota(jnp.int32, (pairs, LANES), 1) < NB
    for source, target in ((result, result_out), (final, final_out)):
        flat = source.reshape(pairs * CASES, LANES)
        for pair in range(CASES // 2):
            even = flat[pl.ds(2 * pair, pairs, stride=CASES), :]
            odd = flat[pl.ds(2 * pair + 1, pairs, stride=CASES), :]
            stage[pl.ds(pair * block_rows, pairs, stride=2), :] = jnp.where(left, even, pltpu.roll(odd, NB, 1))
            stage[pl.ds(pair * block_rows + 1, pairs, stride=2), :] = jnp.where(left, pltpu.roll(even, NB, 1), odd)
        for pair in range(CASES // 2):
            target[:, pair * LANES:(pair + 1) * LANES] = stage[pair * block_rows:(pair + 1) * block_rows]
    interior_out[...] = interior[...]


def body(interface_load, schur_values, schur_columns, coupling, layer_inverse, interior_load, adjacency, live_counts):
    block_rows = interface_load.shape[0]
    slots = schur_columns.shape[1]
    members = lax.axis_size("member")
    regions = lax.axis_size("region")
    outer = 4 if members % 4 == 0 else members
    inner = members // outer
    pairs = block_rows // 2
    groups = schur_values.shape[2] // LANES
    subs, size = interior_load.shape[0], interior_load.shape[2]
    packed = (pairs, CASES, LANES)
    smem = pl.BlockSpec(memory_space=pltpu.SMEM)
    vmem = pl.BlockSpec(memory_space=pltpu.VMEM)
    anywhere = pl.BlockSpec(memory_space=pl.ANY)
    dma = pltpu.SemaphoreType.DMA
    result, final, interior = pl.pallas_call(
        functools.partial(fused_kernel, regions, outer, inner),
        out_shape=(
            jax.ShapeDtypeStruct(packed, F32),
            jax.ShapeDtypeStruct(packed, F32),
            jax.ShapeDtypeStruct(interior_load.shape, F32),
        ),
        in_specs=[smem, smem, smem, vmem, vmem, anywhere, anywhere, anywhere],
        out_specs=(vmem, vmem, vmem),
        scratch_shapes=[
            pltpu.VMEM((3 * members * pairs, CASES, LANES), F32),
            pltpu.VMEM((3 * members * pairs, CASES, LANES), F32),
            pltpu.VMEM(packed, F32),
            pltpu.VMEM(packed, F32),
            pltpu.VMEM((block_rows, slots // 8, groups, 8, LANES), F32),
            pltpu.VMEM((block_rows, 4 * groups, slots * NB), BF16),
            pltpu.VMEM((4, 2 * CASES, slots * NB), BF16),
            pltpu.VMEM((2, pairs, CASES, 4 * groups), F32),
            pltpu.VMEM(coupling.shape, F32),
            pltpu.VMEM(coupling.shape, BF16),
            pltpu.VMEM(coupling.shape, BF16),
            pltpu.VMEM(layer_inverse.shape, F32),
            pltpu.VMEM(layer_inverse.shape, BF16),
            pltpu.VMEM(layer_inverse.shape, BF16),
            pltpu.VMEM((4, subs, CASES, size), F32),
            pltpu.VMEM((2, members, CASES, LANES), F32),
            pltpu.VMEM((2, regions, CASES, LANES), F32),
            dma((slots // 8, groups)),
            dma((2,)),
            dma((2, 3, outer, inner)),
            dma((2, outer)),
            dma((2, outer, inner)),
            dma((2, 2, outer, inner)),
            dma((2, members)),
            dma((2, members)),
            dma((2, regions)),
            dma((2, regions)),
        ],
        compiler_params=pltpu.CompilerParams(
            collective_id=0, has_side_effects=True, vmem_limit_bytes=56 * 2**20
        ),
    )(schur_columns, adjacency, live_counts, interface_load, interior_load, schur_values, coupling, layer_inverse)

    return pl.pallas_call(
        unpack_kernel,
        out_shape=(
            jax.ShapeDtypeStruct(interface_load.shape, F32),
            jax.ShapeDtypeStruct(interface_load.shape, F32),
            jax.ShapeDtypeStruct(interior_load.shape, F32),
        ),
        in_specs=[vmem] * 3,
        out_specs=(vmem,) * 3,
        scratch_shapes=[pltpu.VMEM((pairs * CASES, LANES), F32)],
    )(result, final, interior)


def solution(mesh):
    in_specs = (
        P(("region", "member"), None),
        P(("region", "member"), None, None),
        P(("region", "member"), None),
        P(("region", "member"), None, None),
        P(("region", "member"), None, None),
        P(("region", "member"), None, None),
        P(("region", "member"), None),
        P(("region", "member")),
    )
    out_specs = (
        P(("region", "member"), None),
        P(("region", "member"), None),
        P(("region", "member"), None, None),
    )
    return jax.shard_map(body, mesh=mesh, in_specs=in_specs, out_specs=out_specs, check_vma=False)
```

```python
import functools

import jax
import jax.numpy as jnp
from jax import lax
from jax.experimental import pallas as pl
from jax.experimental.pallas import tpu as pltpu
from jax.sharding import PartitionSpec as P

NB = 64
CASES = 16
LANES = 2 * NB
MESH = pl.DeviceIdType.MESH
F32 = jnp.float32
BF16 = jnp.bfloat16


def split(value):
    high = value.astype(BF16)
    return high, (value - high.astype(F32)).astype(BF16)


def dot_rows(left, right, precision=None):
    return lax.dot_general(left, right, (((1,), (1,)), ((), ())), precision=precision, preferred_element_type=F32)


def fused_kernel(regions, outer, inner, cols, adj, live, given_ref, iload_ref, values_hbm, coupling_hbm, inverse_hbm,
                 result_ref, final_ref, interior_ref,
                 win_load, win_image, load_ref, second_ref, tiles_ref, values_ref, xx, raw, coup, coup_h, coup_l, inv, inv_h, inv_l, base, parts, rows,
                 value_sem, big_sem, recv_sem, line_sem, side_sem, region_sem,
                 member_send, member_recv, row_send, row_recv):
    members = outer * inner
    windows = (win_load, win_image)
    block_rows = cols.shape[0]
    slots = cols.shape[1]
    pairs = block_rows // 2
    subs, interior_size = iload_ref.shape[0], iload_ref.shape[2]
    groups = values_hbm.shape[2] // LANES
    octets = slots // 8
    g = lax.axis_index("region")
    m = lax.axis_index("member")
    a = m // inner
    b = m % inner
    has_low = g > 0
    has_high = g < regions - 1
    barrier = pltpu.get_barrier_semaphore()
    lane = lax.broadcasted_iota(jnp.int32, (CASES, LANES), 1)
    upper = lane // NB

    def value_copy(octet, group):
        return pltpu.make_async_copy(
            values_hbm.at[:, pl.ds(octet * 8, 8), pl.ds(pl.multiple_of(group * LANES, LANES), LANES)],
            tiles_ref.at[:, octet, group], value_sem.at[octet, group])

    def greet(region, member):
        pl.semaphore_signal(barrier, inc=1, device_id=(region, member), device_id_type=MESH)

    for step in range(1, members):
        greet(g, lax.rem(m + step, members))
    for step in range(1, regions):
        greet(lax.rem(g + step, regions), m)

    for octet in range(octets):
        def start_values(group, carry):
            value_copy(octet, group).start()
            return carry
        lax.fori_loop(0, groups, start_values, 0)
    big = [pltpu.make_async_copy(coupling_hbm, coup, big_sem.at[0]),
           pltpu.make_async_copy(inverse_hbm, inv, big_sem.at[1])]
    def remote(source, target, send, recv, region, member):
        return pltpu.make_async_remote_copy(
            src_ref=source, dst_ref=target, send_sem=send, recv_sem=recv,
            device_id=(region, member), device_id_type=MESH,
        )

    half_size = pairs // 2
    halves = range(2)

    def slot(turn, rel, row, column, half):
        first = ((rel * outer + row) * inner + column) * pairs + half * half_size
        return windows[turn].at[pl.ds(first, half_size)]

    def line_copy(turn, step, half):
        here = slot(turn, 1, a, b, half)
        return remote(here, here, line_sem.at[turn, step, half], recv_sem.at[turn, 1, a, b, half],
                      g, lax.rem(a + step, outer) * inner + b)

    def side_copy(turn, row, step, half):
        here = slot(turn, 1, row, b, half)
        return remote(here, here, side_sem.at[turn, row, step, half], recv_sem.at[turn, 1, row, b, half],
                      g, a * inner + lax.rem(b + step, inner))

    def region_copy(turn, row, column, up, half):
        rel = 0 if up else 2
        return remote(slot(turn, 1, row, column, half), slot(turn, rel, row, column, half),
                      region_sem.at[turn, rel // 2, row, column, half],
                      recv_sem.at[turn, rel, row, column, half], g + 1 if up else g - 1, m)

    def spread_regions(turn, row, column, half):
        @pl.when(has_high)
        def _():
            region_copy(turn, row, column, True, half).start()

        @pl.when(has_low)
        def _():
            region_copy(turn, row, column, False, half).start()

    def await_slot(turn, rel, row, column, half):
        here = slot(turn, rel, row, column, half)
        remote(here, here, line_sem.at[turn, 0, half], recv_sem.at[turn, rel, row, column, half], g, m).wait_recv()

    def send_own(turn, half):
        for step in range(1, outer):
            line_copy(turn, step, half).start()
        for step in range(1, inner):
            side_copy(turn, a, step, half).start()
        spread_regions(turn, a, b, half)

    def forward_line(turn, step):
        row = lax.rem(a + outer - step, outer)
        for half in halves:
            await_slot(turn, 1, row, b, half)
            for side in range(1, inner):
                side_copy(turn, row, side, half).start()
            spread_regions(turn, row, b, half)

    def forward_side(turn, step):
        row = lax.rem(a + outer - step, outer)
        for side in range(1, inner):
            column = lax.rem(b + inner - side, inner)
            for half in halves:
                await_slot(turn, 1, row, column, half)
                spread_regions(turn, row, column, half)

    def forward_all(turn, work, skip):
        work = list(work)
        count = 2 * outer - 1
        for place in range(count):
            if place % 2:
                forward_line(turn, (place + 1) // 2)
            else:
                forward_side(turn, place // 2)
            if place >= skip:
                first, after = ((place + more - skip) * len(work) // (count - skip) for more in range(2))
                for item in work[first:after]:
                    item()

    def every_block(act):
        for row in range(outer):
            for column in range(inner):
                for half in halves:
                    act(row, column, half)

    def await_regions(turn):
        def act(row, column, half):
            @pl.when(has_low)
            def _():
                await_slot(turn, 0, row, column, half)

            @pl.when(has_high)
            def _():
                await_slot(turn, 2, row, column, half)
        every_block(act)

    def finish_sends(turn):
        def act(row, column, half):
            @pl.when(has_low)
            def _():
                region_copy(turn, row, column, False, half).wait_send()

            @pl.when(has_high)
            def _():
                region_copy(turn, row, column, True, half).wait_send()
        every_block(act)
        for half in halves:
            for step in range(1, outer):
                line_copy(turn, step, half).wait_send()
            for row in range(outer):
                for step in range(1, inner):
                    side_copy(turn, row, step, half).wait_send()

    def member_copy(turn, step):
        here = parts.at[turn, m]
        return remote(here, here, member_send.at[turn, step], member_recv.at[turn, m], g, lax.rem(m + step, members))

    def row_copy(turn, step):
        here = rows.at[turn, g]
        return remote(here, here, row_send.at[turn, step], row_recv.at[turn, g], lax.rem(g + step, regions), m)

    def sum_start(turn, products):
        packed = jnp.zeros((CASES, LANES), F32)
        for place, product in enumerate(products):
            packed = jnp.where(lane == place, jnp.sum(product, axis=1, keepdims=True), packed)
        parts[turn, m] = packed
        for step in range(1, members):
            member_copy(turn, step).start()

    def sum_middle(turn):
        for step in range(1, members):
            other = lax.rem(m + step, members)
            here = parts.at[turn, other]
            remote(here, here, member_send.at[turn, 0], member_recv.at[turn, other], g, other).wait_recv()
        total = parts[turn, 0]
        for other in range(1, members):
            total = total + parts[turn, other]
        rows[turn, g] = total
        for step in range(1, regions):
            row_copy(turn, step).start()

    def sum_end(turn, count):
        for step in range(1, regions):
            other = lax.rem(g + step, regions)
            here = rows.at[turn, other]
            remote(here, here, row_send.at[turn, 0], row_recv.at[turn, other], other, m).wait_recv()
        total = rows[turn, 0]
        for other in range(1, regions):
            total = total + rows[turn, other]
        for step in range(1, members):
            member_copy(turn, step).wait_send()
        for step in range(1, regions):
            row_copy(turn, step).wait_send()
        return [jnp.sum(jnp.where(lane == place, total, 0.0), axis=1, keepdims=True) for place in range(count)]

    first_id = (g - 1) * (block_rows * members)

    def prepare_values(first, count):
        flat = tiles_ref.reshape(block_rows * octets * groups * 8, LANES)
        wide = lax.broadcasted_iota(jnp.int32, (groups, LANES), 1) // NB

        def one(i, carry):
            for k in range(0, slots, 2):
                start = (i * octets + k // 8) * (groups * 8) + k % 8
                first_slot = flat[pl.ds(start, groups, stride=8), :]
                second_slot = flat[pl.ds(start + 1, groups, stride=8), :]
                place = slice(k // 2 * LANES, (k // 2 + 1) * LANES)
                for p, joined in enumerate((jnp.where(wide == 0, first_slot, pltpu.roll(second_slot, NB, 1)),
                                            jnp.where(wide == 0, pltpu.roll(first_slot, NB, 1), second_slot))):
                    high, low = split(joined)
                    values_ref[i, p * groups:(p + 1) * groups, place] = high
                    values_ref[i, (2 + p) * groups:(3 + p) * groups, place] = low
            return carry
        lax.fori_loop(first, first + count, one, 0)

    def await_values():
        for octet in range(octets):
            def wait_values(group, carry):
                value_copy(octet, group).wait()
                return carry
            lax.fori_loop(0, groups, wait_values, 0)

    def doubled(fetch, block):
        local = jnp.clip(block - first_id, 0, 3 * members * block_rows - 1)
        tile = fetch(lax.shift_right_logical(local, 1))
        kept = jnp.where(upper == lax.bitwise_and(local, 1), tile, 0.0)
        return kept + pltpu.roll(kept, NB, 1)

    def apply_schur(fetch, start, count):
        def four(u, carry):
            for j in range(4):
                i = 4 * u + j
                for k in range(0, slots, 2):
                    place = slice(k // 2 * LANES, (k // 2 + 1) * LANES)
                    high, low = split(jnp.where(upper == 0, doubled(fetch, cols[i, k]), doubled(fetch, cols[i, k + 1])))
                    xx[j, 0:CASES, place] = high
                    xx[j, CASES:2 * CASES, place] = low
                product = dot_rows(xx[j], values_ref[i])
                raw[j % 2, 2 * u + j // 2] = product[0:CASES] + product[CASES:2 * CASES]
            return carry
        lax.fori_loop(start // 2, (start + count) // 2, four, 0)
        place = lax.broadcasted_iota(jnp.int32, (LANES, 8 * groups), 0)
        source = lax.broadcasted_iota(jnp.int32, (LANES, 8 * groups), 1)
        target = source // (4 * groups) * NB + 2 * (source % groups) + source // groups % 2
        chosen = jnp.where(place == target, 1.0, 0.0).astype(BF16)
        joined = jnp.concatenate([raw[parity, start:start + count].reshape(count * CASES, 4 * groups) for parity in range(2)], axis=1)
        high = joined.astype(BF16)
        rest = joined - high.astype(F32)
        middle, low = split(rest)
        total = dot_rows(high, chosen) + (dot_rows(middle, chosen) + dot_rows(low, chosen))
        return total.reshape(count, CASES, LANES)

    def prepare_recovery(source, high_ref, low_ref, s, part):
        def one(chunk, carry):
            piece = pl.ds(pl.multiple_of(chunk * 64, 64), 64)
            high, low = split(source[s, piece, :])
            high_ref[s, piece, :] = high
            low_ref[s, piece, :] = low
            return carry
        portion = interior_size // 128
        lax.fori_loop(part * portion, (part + 1) * portion, one, 0)

    def multiply(values, high_ref, low_ref, s, chunks=None):
        parted = [split(value) for value in values]
        count = len(values) * CASES
        highs = jnp.concatenate([high for high, _ in parted], axis=0)
        stacked = jnp.concatenate([highs] + [low for _, low in parted], axis=0)
        pieces = []
        for chunk in chunks or range(interior_size // 256):
            piece = slice(chunk * 256, (chunk + 1) * 256)
            product = dot_rows(stacked, high_ref[s, piece, :])
            pieces.append(product[0:count] + product[count:2 * count] + dot_rows(highs, low_ref[s, piece, :]))
        return jnp.concatenate(pieces, axis=1)

    def picked(fetch, s):
        pieces = []
        for pair in range(adj.shape[1] // 2):
            halves = []
            for side in range(2):
                slot_id = 2 * pair + side
                both = doubled(fetch, adj[s, slot_id])
                halves.append(jnp.where(jnp.full((CASES, LANES), live[s]) > slot_id, both, 0.0))
            pieces.append(jnp.where(upper == 0, halves[0], halves[1]))
        return jnp.concatenate(pieces, axis=1)

    def coupled(fetch, s):
        return multiply([picked(fetch, s)], coup_h, coup_l, s)

    own = (members + m) * pairs
    load_flat = load_ref.reshape(pairs * CASES, LANES)
    stage = second_ref.reshape(pairs * CASES, LANES)
    left = lax.broadcasted_iota(jnp.int32, (pairs, LANES), 1) < NB
    for pair in range(CASES // 2):
        stage[pair * block_rows:(pair + 1) * block_rows] = given_ref[:, pair * LANES:(pair + 1) * LANES]
    for pair in range(CASES // 2):
        even = stage[pl.ds(pair * block_rows, pairs, stride=2), :]
        odd = stage[pl.ds(pair * block_rows + 1, pairs, stride=2), :]
        load_flat[pl.ds(2 * pair, pairs, stride=CASES), :] = jnp.where(left, even, pltpu.roll(odd, NB, 1))
        load_flat[pl.ds(2 * pair + 1, pairs, stride=CASES), :] = jnp.where(left, pltpu.roll(even, NB, 1), odd)
    win_load[pl.ds(own, pairs)] = load_ref[...]
    pl.semaphore_wait(barrier, members - 1 + regions - 1)
    for half in halves:
        send_own(0, half)

    def operands_here():
        await_values()
        for copy in big:
            copy.start()

    part_rows = block_rows // 8
    pieces = [functools.partial(prepare_values, first, part_rows) for first in range(0, block_rows, part_rows)]
    forward_all(0, [operands_here] + pieces, 2)
    await_regions(0)

    def fetch_load(tile):
        return win_load[tile]

    load = load_ref[...]
    images = []
    for half in halves:
        images.append(apply_schur(fetch_load, half * half_size, half_size))
        win_image[pl.ds(own + half * half_size, half_size)] = images[half]
        send_own(1, half)
    image = jnp.concatenate(images, axis=0)
    sum_start(0, [jnp.sum(load * load, axis=0), jnp.sum(load * image, axis=0)])

    def big_here():
        for copy in big:
            copy.wait()

    def couple_known(s):
        base[3, s] = coupled(fetch_load, s)

    def solve_known(s, chunk):
        both = multiply([iload_ref[s], base[3, s]], inv_h, inv_l, s, (chunk,))
        place = slice(chunk * 256, (chunk + 1) * 256)
        base[0, s, :, place] = both[0:CASES]
        base[1, s, :, place] = both[CASES:2 * CASES]

    work = [big_here]
    for source, high_ref, low_ref in ((coup, coup_h, coup_l), (inv, inv_h, inv_l)):
        work += [functools.partial(prepare_recovery, source, high_ref, low_ref, s, part)
                 for s in range(subs) for part in range(2)]
    work.insert(len(work) // 2, functools.partial(sum_middle, 0))
    work += [functools.partial(couple_known, s) for s in range(subs)]
    work += [functools.partial(solve_known, s, chunk) for s in range(subs) for chunk in range(interior_size // 256)]
    late = len(work) // 3
    forward_all(1, work[:-late], 0)
    for item in work[-late:]:
        item()
    norm, curve = sum_end(0, 2)
    step = norm / curve
    await_regions(1)

    def fetch_residual(tile):
        return win_load[tile] - step * win_image[tile]

    second = apply_schur(fetch_residual, 0, pairs)
    residual = load - step * image
    second_ref[...] = second
    sum_start(1, [jnp.sum(residual * residual, axis=0), jnp.sum(residual * second, axis=0),
                  jnp.sum(residual * image + load * second, axis=0)])
    for s in range(subs):
        base[2, s] = multiply([coupled(fetch_residual, s)], inv_h, inv_l, s)
        if s == 0:
            sum_middle(1)
    norm_next, square, cross = sum_end(1, 3)
    ratio = norm_next / norm
    step_two = norm_next / (square + ratio * (cross + ratio * curve))
    along = step + step_two * ratio
    result_ref[...] = along * load + step_two * residual
    final_ref[...] = residual - step_two * (second_ref[...] + ratio * image)
    for s in range(subs):
        interior_ref[s] = base[0, s] - along * base[1, s] - step_two * base[2, s]
    finish_sends(0)
    finish_sends(1)


def unpack_kernel(result, final, interior, result_out, final_out, interior_out, stage):
    pairs = result.shape[0]
    block_rows = 2 * pairs
    left = lax.broadcasted_iota(jnp.int32, (pairs, LANES), 1) < NB
    for source, target in ((result, result_out), (final, final_out)):
        flat = source.reshape(pairs * CASES, LANES)
        for pair in range(CASES // 2):
            even = flat[pl.ds(2 * pair, pairs, stride=CASES), :]
            odd = flat[pl.ds(2 * pair + 1, pairs, stride=CASES), :]
            stage[pl.ds(pair * block_rows, pairs, stride=2), :] = jnp.where(left, even, pltpu.roll(odd, NB, 1))
            stage[pl.ds(pair * block_rows + 1, pairs, stride=2), :] = jnp.where(left, pltpu.roll(even, NB, 1), odd)
        for pair in range(CASES // 2):
            target[:, pair * LANES:(pair + 1) * LANES] = stage[pair * block_rows:(pair + 1) * block_rows]
    interior_out[...] = interior[...]


def body(interface_load, schur_values, schur_columns, coupling, layer_inverse, interior_load, adjacency, live_counts):
    block_rows = interface_load.shape[0]
    slots = schur_columns.shape[1]
    members = lax.axis_size("member")
    regions = lax.axis_size("region")
    outer = 4 if members % 4 == 0 else members
    inner = members // outer
    pairs = block_rows // 2
    groups = schur_values.shape[2] // LANES
    subs, size = interior_load.shape[0], interior_load.shape[2]
    packed = (pairs, CASES, LANES)
    smem = pl.BlockSpec(memory_space=pltpu.SMEM)
    vmem = pl.BlockSpec(memory_space=pltpu.VMEM)
    anywhere = pl.BlockSpec(memory_space=pl.ANY)
    dma = pltpu.SemaphoreType.DMA
    result, final, interior = pl.pallas_call(
        functools.partial(fused_kernel, regions, outer, inner),
        out_shape=(
            jax.ShapeDtypeStruct(packed, F32),
            jax.ShapeDtypeStruct(packed, F32),
            jax.ShapeDtypeStruct(interior_load.shape, F32),
        ),
        in_specs=[smem, smem, smem, vmem, vmem, anywhere, anywhere, anywhere],
        out_specs=(vmem, vmem, vmem),
        scratch_shapes=[
            pltpu.VMEM((3 * members * pairs, CASES, LANES), F32),
            pltpu.VMEM((3 * members * pairs, CASES, LANES), F32),
            pltpu.VMEM(packed, F32),
            pltpu.VMEM(packed, F32),
            pltpu.VMEM((block_rows, slots // 8, groups, 8, LANES), F32),
            pltpu.VMEM((block_rows, 4 * groups, slots * NB), BF16),
            pltpu.VMEM((4, 2 * CASES, slots * NB), BF16),
            pltpu.VMEM((2, pairs, CASES, 4 * groups), F32),
            pltpu.VMEM(coupling.shape, F32),
            pltpu.VMEM(coupling.shape, BF16),
            pltpu.VMEM(coupling.shape, BF16),
            pltpu.VMEM(layer_inverse.shape, F32),
            pltpu.VMEM(layer_inverse.shape, BF16),
            pltpu.VMEM(layer_inverse.shape, BF16),
            pltpu.VMEM((4, subs, CASES, size), F32),
            pltpu.VMEM((2, members, CASES, LANES), F32),
            pltpu.VMEM((2, regions, CASES, LANES), F32),
            dma((slots // 8, groups)),
            dma((2,)),
            dma((2, 3, outer, inner, 2)),
            dma((2, outer, 2)),
            dma((2, outer, inner, 2)),
            dma((2, 2, outer, inner, 2)),
            dma((2, members)),
            dma((2, members)),
            dma((2, regions)),
            dma((2, regions)),
        ],
        compiler_params=pltpu.CompilerParams(
            collective_id=0, has_side_effects=True, vmem_limit_bytes=56 * 2**20
        ),
    )(schur_columns, adjacency, live_counts, interface_load, interior_load, schur_values, coupling, layer_inverse)

    return pl.pallas_call(
        unpack_kernel,
        out_shape=(
            jax.ShapeDtypeStruct(interface_load.shape, F32),
            jax.ShapeDtypeStruct(interface_load.shape, F32),
            jax.ShapeDtypeStruct(interior_load.shape, F32),
        ),
        in_specs=[vmem] * 3,
        out_specs=(vmem,) * 3,
        scratch_shapes=[pltpu.VMEM((pairs * CASES, LANES), F32)],
    )(result, final, interior)


def solution(mesh):
    in_specs = (
        P(("region", "member"), None),
        P(("region", "member"), None, None),
        P(("region", "member"), None),
        P(("region", "member"), None, None),
        P(("region", "member"), None, None),
        P(("region", "member"), None, None),
        P(("region", "member"), None),
        P(("region", "member")),
    )
    out_specs = (
        P(("region", "member"), None),
        P(("region", "member"), None),
        P(("region", "member"), None, None),
    )
    return jax.shard_map(body, mesh=mesh, in_specs=in_specs, out_specs=out_specs, check_vma=False)
```
